32 devices in a mesh: dp: 16 (over z, y, core), fsdp: 2 (over x).
Axes of the slice: x: 2, y: 2, z: 4, core: 2. Of those that a mesh axis runs over, the one named last changes fastest.
Arguments:
- tokens: bfloat16 [16384, 960], P(('dp', 'fsdp')), may hold values from -6 to 6
- segments: int32 [16384], P(('dp', 'fsdp')), may hold values from 0 to 63, as said below
- cotangent: bfloat16 [16384, 960], P(('dp', 'fsdp')), may hold values from -6 to 6
- attn_gain: bfloat16 [960], P('fsdp'), may hold values from 0.5 to 1.5
- w_query: bfloat16 [960, 960], P('fsdp'), may hold values from -0.1875 to 0.1875
- w_key: bfloat16 [960, 320], P('fsdp'), may hold values from -0.1875 to 0.1875
- w_value: bfloat16 [960, 320], P('fsdp'), may hold values from -0.1875 to 0.1875
- w_out: bfloat16 [960, 960], P('fsdp'), may hold values from -0.75 to 0.75
- mlp_gain: bfloat16 [960], P('fsdp'), may hold values from 0.5 to 1.5
- w_gate: bfloat16 [960, 2560], P('fsdp'), may hold values from -0.1875 to 0.1875
- w_up: bfloat16 [960, 2560], P('fsdp'), may hold values from -0.1875 to 0.1875
- w_down: bfloat16 [2560, 960], P('fsdp'), may hold values from -0.125 to 0.125
Outputs:
- activations: bfloat16 [16384, 960], P(('dp', 'fsdp'))
- input_grad: float32 [16384, 960], P(('dp', 'fsdp'))
- attn_gain_grad: float32 [960], P('fsdp')
- query_grad: float32 [960, 960], P('fsdp')
- key_grad: float32 [960, 320], P('fsdp')
- value_grad: float32 [960, 320], P('fsdp')
- out_grad: float32 [960, 960], P('fsdp')
- mlp_gain_grad: float32 [960], P('fsdp')
- gate_grad: float32 [960, 2560], P('fsdp')
- up_grad: float32 [960, 2560], P('fsdp')
- down_grad: float32 [2560, 960], P('fsdp')
The draws below stay inside these ranges and needn't reach their ends.
Inputs may be any that keep to these rules, and one draw needn't show every extreme that they name: `segments`: rows fall into aligned blocks of 512; in each block the id is 0 at its first row and rises by 0 or 1 from one row to the next, rising only at rows whose place in the block is a multiple of 8, so every sequence is a multiple of 8 rows long. In every draw some block holds a single sequence of all 512 rows.
All inputs are finite; a program needn't handle non-finite values.
Results may differ from the reference program's by a relative error of at most 0.022.
Values may be sent and summed in bfloat16 or wider, within the bound.
A program may use at most 384 MiB of HBM per device.

```python
import jax
import jax.numpy as jnp
from jax import lax

D = 960
HEADS = 15
KV_HEADS = 5
HEAD = 64
FF = 2560
TOK_DEV = 512
TOKENS = 16384


def draw_segments(key, part):
    key = jax.random.fold_in(key, 11)
    blocks = TOKENS // TOK_DEV
    rate_key, flag_key, pick_key = jax.random.split(key, 3)
    exponents = jax.random.randint(rate_key, (blocks, 1), 0, 6)
    single = jax.random.randint(pick_key, (), 0, blocks)
    dense = (single + 1) % blocks
    block_index = jnp.arange(blocks)[:, None]
    exponents = jnp.where(block_index == dense, 0, exponents)
    spacing = jnp.left_shift(jnp.int32(1), exponents)
    numbers = jax.random.randint(flag_key, (blocks, TOK_DEV), 0, 1 << 30)
    places = jnp.arange(TOK_DEV)
    starts = (numbers % spacing == 0) & (places[None, :] % 8 == 0)
    starts = jnp.where(block_index == single, False, starts)
    starts = starts | (places[None, :] == 0)
    segment_ids = jnp.cumsum(starts.astype(jnp.int32), axis=1) - 1
    return segment_ids.reshape(TOKENS).astype(jnp.int32)


def shard_levels(key, dims, cuts, least, high):
    factor_of = 1.0
    for dim, blocks in cuts:
        draws = jax.random.uniform(jax.random.fold_in(jax.random.fold_in(key, 6), dim), (blocks,), jnp.float32, least / len(cuts), high / len(cuts))
        factor_of = factor_of * jnp.repeat(jnp.exp(draws), dims[dim] // blocks).reshape((-1,) + (1,) * (len(dims) - 1 - dim))
    return factor_of


def centred(rng, dims, width, most, pieces=(), held_as=jnp.bfloat16):
    array = width * jax.random.normal(rng, dims, jnp.float32)
    if pieces:
        array = array * shard_levels(rng, dims, pieces, -0.22, 0.18)
    return jnp.clip(array, -most, most).astype(held_as)


def setup_inputs(seed: int = 0) -> dict:
    key_of = jax.random.split(jax.random.key(seed), 13)
    tokens = centred(key_of[0], (TOKENS, D), 1.0, 6.0, ((0, 32),))
    segments = draw_segments(jax.random.fold_in(key_of[12], 71), 0)
    cotangent = centred(key_of[2], (TOKENS, D), 1.0, 6.0, ((0, 32),))
    attn_gain = jnp.clip(1.0 + 0.1 * jax.random.normal(key_of[3], (D,), jnp.float32), 0.5, 1.5).astype(jnp.bfloat16)
    w_query = centred(key_of[4], (D, HEADS * HEAD), D ** -0.5, 0.1875, ((0, 2),))
    w_key = centred(key_of[5], (D, KV_HEADS * HEAD), D ** -0.5, 0.1875, ((0, 2),))
    w_value = centred(key_of[6], (D, KV_HEADS * HEAD), D ** -0.5, 0.1875, ((0, 2),))
    w_out = centred(key_of[7], (HEADS * HEAD, D), (HEADS * HEAD // 16) ** -0.5, 0.75, ((0, 2),))
    mlp_gain = jnp.clip(1.0 + 0.1 * jax.random.normal(key_of[8], (D,), jnp.float32), 0.5, 1.5).astype(jnp.bfloat16)
    w_gate = centred(key_of[9], (D, FF), D ** -0.5, 0.1875, ((0, 2),))
    w_up = centred(key_of[10], (D, FF), D ** -0.5, 0.1875, ((0, 2),))
    w_down = centred(key_of[11], (FF, D), FF ** -0.5, 0.125, ((0, 2),))
    return {"tokens": tokens, "segments": segments, "cotangent": cotangent, "attn_gain": attn_gain, "w_query": w_query, "w_key": w_key, "w_value": w_value, "w_out": w_out, "mlp_gain": mlp_gain, "w_gate": w_gate, "w_up": w_up, "w_down": w_down}


@jax.custom_vjp
def low(v):
    return lax.optimization_barrier(v.astype(jnp.bfloat16)).astype(jnp.float32)

@jax.custom_vjp
def low_back(v):
    return v

def low_keep(v):
    return (low(v), None)

def low_pass(kept, grad):
    return (grad,)

def back_keep(v):
    return (v, None)

def back_low(kept, grad):
    return (low(grad),)
low.defvjp(low_keep, low_pass)
low_back.defvjp(back_keep, back_low)
epsilon = 1e-05
rope_base = 100000.0
masked_score = -1e+30

def rope_tables(segment_ids):
    places = jnp.arange(segment_ids.shape[0], dtype=jnp.int32)
    changed = jnp.concatenate([jnp.ones((1,), dtype=bool), segment_ids[1:] != segment_ids[:-1]])
    first = lax.cummax(jnp.where(changed, places, 0), axis=0)
    position = (places - first).astype(jnp.float32)
    frequency = rope_base ** (-jnp.arange(0, HEAD, 2, dtype=jnp.float32) / HEAD)
    angles = position[:, None] * frequency[None, :]
    angles = jnp.concatenate([angles, angles], axis=1)
    return (jnp.cos(angles), jnp.sin(angles))

def rotate(values, cosine, sine, direction):
    rows_total = values.shape[0]
    shaped = values.reshape(rows_total, -1, HEAD)
    midway = HEAD // 2
    turned = jnp.concatenate([-shaped[..., midway:], shaped[..., :midway]], axis=-1)
    return (shaped * cosine[:, None, :] + direction * turned * sine[:, None, :]).reshape(rows_total, -1)

def matmul(left, right):
    return jnp.dot(left, right, precision=lax.Precision.HIGHEST)

def rms_scale(values):
    return values * lax.rsqrt(lax.optimization_barrier(jnp.mean(values * values, axis=-1, keepdims=True)) + epsilon)

def forward(resid_in, weights, segment_ids, cosine, sine):
    gain_one, query_w, key_w, value_w, out_w, gain_two, gate_w, up_w, down_w = weights
    rows_total = resid_in.shape[0]
    group = HEADS // KV_HEADS
    attn_in = low(rms_scale(resid_in) * gain_one)
    queries = low(rotate(low_back(matmul(attn_in, query_w)), cosine, sine, 1.0))
    keys = low(rotate(low_back(matmul(attn_in, key_w)), cosine, sine, 1.0))
    values = low(low_back(matmul(attn_in, value_w)))
    scores = jnp.einsum('qgrd,kgd->grqk', queries.reshape(rows_total, KV_HEADS, group, HEAD), keys.reshape(rows_total, KV_HEADS, HEAD), precision=lax.Precision.HIGHEST) * HEAD ** (-0.5)
    scores = low_back(scores)
    places = jnp.arange(rows_total)
    allowed = (segment_ids[:, None] == segment_ids[None, :]) & (places[:, None] >= places[None, :])
    scores = jnp.where(allowed, scores, masked_score)
    probability = low(jax.nn.softmax(scores, axis=-1))
    mixed = jnp.einsum('grqk,kgd->qgrd', probability, values.reshape(rows_total, KV_HEADS, HEAD), precision=lax.Precision.HIGHEST).reshape(rows_total, HEADS * HEAD)
    mixed = low(low_back(mixed))
    middle = resid_in + low_back(matmul(mixed, out_w))
    mlp_in = low(rms_scale(middle) * gain_two)
    gate = low_back(matmul(mlp_in, gate_w))
    upward = low_back(matmul(mlp_in, up_w))
    activated = low(jax.nn.silu(gate) * upward)
    return middle + low_back(matmul(activated, down_w))

def reference(tokens, segments, cotangent, attn_gain, w_query, w_key, w_value, w_out, mlp_gain, w_gate, w_up, w_down):
    params = tuple((weight.astype(jnp.float32) for weight in (attn_gain, w_query, w_key, w_value, w_out, mlp_gain, w_gate, w_up, w_down)))
    blocks = tokens.shape[0] // TOK_DEV

    def one_block(accum, items):
        block_in, block_ids, block_grad = items
        cosine, sine = rope_tables(block_ids)

        def run(resid_in, weights):
            return forward(resid_in, weights, block_ids, cosine, sine)
        output, pullback = jax.vjp(run, block_in.astype(jnp.float32), params)
        grad_input, grad_weights = pullback(block_grad.astype(jnp.float32))
        accum = tuple((total + part for total, part in zip(accum, grad_weights)))
        return (accum, (output.astype(jnp.bfloat16), grad_input))
    zeros = tuple((jnp.zeros_like(weight) for weight in params))
    accum, (outputs, input_grads) = lax.scan(one_block, zeros, (tokens.reshape(blocks, TOK_DEV, -1), segments.reshape(blocks, TOK_DEV), cotangent.reshape(blocks, TOK_DEV, -1)))
    return (outputs.reshape(tokens.shape), input_grads.reshape(tokens.shape), accum[0], accum[1], accum[2], accum[3], accum[4], accum[5], accum[6], accum[7], accum[8])
```

```python
import functools

import jax
import jax.numpy as jnp
from jax import lax
from jax.experimental import pallas as pl
from jax.experimental.pallas import tpu as pltpu
from jax.sharding import PartitionSpec as P

HEADS = 15
KV_HEADS = 5
HEAD = 64


epsilon = 1e-05
rope_base = 100000.0
masked_score = -1e30


def rope_tables(segment_ids):
    places = jnp.arange(segment_ids.shape[0], dtype=jnp.int32)
    changed = jnp.concatenate([jnp.ones((1,), dtype=bool), segment_ids[1:] != segment_ids[:-1]])
    first = lax.cummax(jnp.where(changed, places, 0), axis=0)
    position = (places - first).astype(jnp.float32)
    frequency = rope_base ** (-jnp.arange(0, HEAD, 2, dtype=jnp.float32) / HEAD)
    angles = position[:, None] * frequency[None, :]
    angles = jnp.concatenate([angles, angles], axis=1)
    return (jnp.cos(angles), jnp.sin(angles))


def rotate(values, cosine, sine, direction):
    rows_total = values.shape[0]
    shaped = values.reshape(rows_total, -1, HEAD)
    midway = HEAD // 2
    turned = jnp.concatenate([-shaped[..., midway:], shaped[..., :midway]], axis=-1)
    return (shaped * cosine[:, None, :] + direction * turned * sine[:, None, :]).reshape(
        rows_total, -1
    )


def norm_forward(values, gain):
    scale_rows = lax.rsqrt(jnp.mean(values * values, axis=-1, keepdims=True) + epsilon)
    normed = values * scale_rows
    return (normed, scale_rows, (normed * gain.astype(jnp.float32)).astype(jnp.bfloat16))


def norm_backward(grad_scaled, normed, scale_rows, gain):
    gain_grad = jnp.sum(grad_scaled * normed, axis=0)
    grad_normed = grad_scaled * gain.astype(jnp.float32)
    inner = jnp.mean(grad_normed * normed, axis=-1, keepdims=True)
    return (scale_rows * (grad_normed - normed * inner), gain_grad)


def block_mask(segment_ids, first_row, last_row):
    places = jnp.arange(segment_ids.shape[0])
    same = segment_ids[first_row:last_row, None] == segment_ids[None, :last_row]
    causal = places[first_row:last_row, None] >= places[None, :last_row]
    return same & causal


def block_scores(query_block, key_block, allowed):
    scores = jnp.einsum(
        "qrd,kd->rqk", query_block, key_block, preferred_element_type=jnp.float32
    ) * HEAD ** (-0.5)
    return jnp.where(allowed[None], scores, masked_score)


def attend_forward(queries, keys, values, segment_ids):
    rows_total = queries.shape[0]
    block_rows = min(512, rows_total)
    group = HEADS // KV_HEADS
    log_totals = []
    allowed = block_mask(segment_ids, 0, block_rows)
    head_parts = []
    for kv_index in range(KV_HEADS):
        query_block = queries[0:block_rows, kv_index * group * HEAD : (kv_index + 1) * group * HEAD]
        query_block = query_block.reshape(block_rows, group, HEAD)
        key_block = keys[:block_rows, kv_index * HEAD : (kv_index + 1) * HEAD]
        value_block = values[:block_rows, kv_index * HEAD : (kv_index + 1) * HEAD]
        scores = block_scores(query_block, key_block, allowed)
        highest = jnp.max(scores, axis=-1, keepdims=True)
        exponent = jnp.exp(scores - highest)
        totals = jnp.sum(exponent, axis=-1, keepdims=True)
        probability = (exponent / totals).astype(jnp.bfloat16)
        log_totals.append(highest + jnp.log(totals))
        mixed = jnp.einsum(
            "rqk,kd->qrd", probability, value_block, preferred_element_type=jnp.float32
        )
        head_parts.append(mixed.reshape(block_rows, group * HEAD))
    mixed_rows = jnp.concatenate(head_parts, axis=1)
    return (mixed_rows, log_totals)


def attend_backward(queries, keys, values, grad_mixed, segment_ids, log_totals):
    rows_total = queries.shape[0]
    block_rows = min(512, rows_total)
    group = HEADS // KV_HEADS
    key_grads = [jnp.zeros((rows_total, HEAD), jnp.float32) for kv_index in range(KV_HEADS)]
    value_grads = [jnp.zeros((rows_total, HEAD), jnp.float32) for kv_index in range(KV_HEADS)]
    entry = 0
    allowed = block_mask(segment_ids, 0, block_rows)
    head_parts = []
    for kv_index in range(KV_HEADS):
        columns_lo = kv_index * group * HEAD
        columns_hi = (kv_index + 1) * group * HEAD
        query_block = queries[0:block_rows, columns_lo:columns_hi].reshape(block_rows, group, HEAD)
        grad_block = grad_mixed[0:block_rows, columns_lo:columns_hi].reshape(
            block_rows, group, HEAD
        )
        key_block = keys[:block_rows, kv_index * HEAD : (kv_index + 1) * HEAD]
        value_block = values[:block_rows, kv_index * HEAD : (kv_index + 1) * HEAD]
        scores = block_scores(query_block, key_block, allowed)
        probability = jnp.exp(scores - log_totals[entry])
        entry = entry + 1
        grad_prob = jnp.einsum(
            "qrd,kd->rqk", grad_block, value_block, preferred_element_type=jnp.float32
        )
        weighted = jnp.sum(probability * grad_prob, axis=-1, keepdims=True)
        grad_scores = (probability * (grad_prob - weighted)).astype(jnp.bfloat16)
        grad_query = jnp.einsum(
            "rqk,kd->qrd", grad_scores, key_block, preferred_element_type=jnp.float32
        ) * HEAD ** (-0.5)
        head_parts.append(grad_query.reshape(block_rows, group * HEAD))
        grad_key = jnp.einsum(
            "rqk,qrd->kd", grad_scores, query_block, preferred_element_type=jnp.float32
        ) * HEAD ** (-0.5)
        grad_value = jnp.einsum(
            "rqk,qrd->kd",
            probability.astype(jnp.bfloat16),
            grad_block,
            preferred_element_type=jnp.float32,
        )
        key_grads[kv_index] = grad_key
        value_grads[kv_index] = grad_value
    grad_query_rows = jnp.concatenate(head_parts, axis=1)
    return (
        grad_query_rows,
        jnp.concatenate(key_grads, axis=1),
        jnp.concatenate(value_grads, axis=1),
    )


def product(left, right):
    return jnp.dot(left, right, preferred_element_type=jnp.float32)


MESH = pl.DeviceIdType.MESH
TALL_CUTS = 2
WIDE_CUTS = 3
PIECE_ROWS = 80


def place():
    dp = lax.axis_index("dp")
    fs = lax.axis_index("fsdp")
    bits = [lax.rem(lax.div(dp, 1 << shift), 2) for shift in range(4)]
    flips = [dp + (1 << shift) - (2 << shift) * bits[shift] for shift in range(4)]
    across = (dp, 1 - fs)
    core, along_y, near_z, far_z = [(flip, fs) for flip in flips]
    return fs, bits, across, core, along_y, near_z, far_z


def greet(partners):
    barrier = pltpu.get_barrier_semaphore()
    for partner in partners:
        pl.semaphore_signal(barrier, inc=1, device_id=partner, device_id_type=MESH)
    pl.semaphore_wait(barrier, len(partners))


def aligned(value, unit):
    return pl.multiple_of(value, unit)


def gather_kernel(
    wide_a, wide_b, wide_c, tall, gains,
    full_a, full_b, full_c, full_tall, full_gains,
    local_sems, send_sems, recv_sems,
):
    fs, bits, across, core, along_y, _, _ = place()
    c, y = bits[0], bits[1]
    shards = (wide_a, wide_b, wide_c, tall)
    fulls = (full_a, full_b, full_c, full_tall)

    def send(src, dst, stage, index, target):
        copy = pltpu.make_async_remote_copy(
            src_ref=src, dst_ref=dst, send_sem=send_sems.at[stage, index],
            recv_sem=recv_sems.at[stage, index], device_id=target, device_id_type=MESH,
        )
        copy.start()
        return copy

    def quarter(ref, index, base, cut):
        rows = shards[index].shape[0]
        half = rows // 2
        if index == 3:
            at = aligned(base * rows + c * half + cut * (half // 2), 16)
            return ref.at[pl.ds(at, half // 2), :]
        columns = shards[index].shape[1] // 2
        at = aligned(base * rows + c * half, 16)
        return ref.at[pl.ds(at, half), pl.ds(aligned(cut * columns, 128), columns)]

    def half_of(ref, index, base):
        rows = shards[index].shape[0]
        at = aligned(base * rows + c * (rows // 2), 16)
        return ref.at[pl.ds(at, rows // 2), :]

    greet((across, core, along_y))
    pending = []
    first = [send(gains, full_gains.at[fs], 0, 4, across)]
    for index in range(4):
        first.append(
            send(
                quarter(shards[index], index, 0, y),
                quarter(fulls[index], index, fs, y), 0, index, across,
            )
        )
    locals_ = [pltpu.make_async_copy(gains, full_gains.at[fs], local_sems.at[4])]
    for index in range(4):
        rows = shards[index].shape[0]
        locals_.append(
            pltpu.make_async_copy(
                shards[index],
                fulls[index].at[pl.ds(aligned(fs * rows, 16), rows), :],
                local_sems.at[index],
            )
        )
    for copy in locals_:
        copy.start()
    first[0].wait_recv()
    second = [None] * 4
    third = [None] * 4
    for step in range(5):
        if step < 4:
            first[step + 1].wait_recv()
            got = quarter(fulls[step], step, 1 - fs, y)
            second[step] = send(got, got, 1, step, along_y)
        if step >= 1:
            index = step - 1
            second[index].wait_recv()
            got = half_of(fulls[index], index, 1 - fs)
            third[index] = send(got, got, 2, index, core)
    for copy in third:
        copy.wait_recv()
    for copy in first + second + third:
        copy.wait_send()
    for copy in locals_:
        copy.wait()


def gather_all(wide_a, wide_b, wide_c, tall, gains):
    def doubled(shard):
        return jax.ShapeDtypeStruct((2 * shard.shape[0], shard.shape[1]), shard.dtype)

    anywhere = pl.BlockSpec(memory_space=pl.ANY)
    return pl.pallas_call(
        gather_kernel,
        out_shape=(
            doubled(wide_a), doubled(wide_b), doubled(wide_c), doubled(tall),
            jax.ShapeDtypeStruct((2,) + gains.shape, gains.dtype),
        ),
        in_specs=[anywhere] * 5,
        out_specs=(anywhere,) * 5,
        scratch_shapes=[
            pltpu.SemaphoreType.DMA((5,)),
            pltpu.SemaphoreType.DMA((3, 5)),
            pltpu.SemaphoreType.DMA((3, 5)),
        ],
        compiler_params=pltpu.CompilerParams(collective_id=0, has_side_effects=True),
    )(wide_a, wide_b, wide_c, tall, gains)


def reduce_kernel(
    tall, wide_a, wide_b, wide_c, gains,
    sum_tall, sum_a, sum_b, sum_c, sum_gains,
    own_t, core_t, across_t, y_t, near_t, far_t, done_t,
    own_w, core_w, across_w, y_w, near_w, far_w, done_w,
    gain_acc, gain_got, load_sems, store_sems, send_sems, recv_sems, gain_sems,
):
    fs, bits, across, core, along_y, near_z, far_z = place()
    c, y, z = bits[0], bits[1], bits[2]
    mine = 2 * y + z
    sources = (tall, wide_a, wide_b, wide_c)
    sinks = (sum_tall, sum_a, sum_b, sum_c)
    chunks = [(0, cut) for cut in range(TALL_CUTS)]
    chunks = chunks + [(1 + i, cut) for i in range(3) for cut in range(WIDE_CUTS)]
    count = len(chunks)

    def buffers(j):
        if j < TALL_CUTS:
            refs, i = (own_t, core_t, across_t, y_t, near_t, far_t, done_t), j
        else:
            refs, i = (own_w, core_w, across_w, y_w, near_w, far_w, done_w), j - TALL_CUTS
        return [ref.at[i] for ref in refs]

    held = [buffers(j) for j in range(count)]

    def piece(ref, which, cut, shard, half, q):
        if which == 0:
            at = shard * 1280 + (cut * 8 + half * 4 + q) * PIECE_ROWS
            return ref.at[pl.ds(at, PIECE_ROWS), :]
        at = shard * 480 + (cut * 2 + half) * PIECE_ROWS
        return ref.at[pl.ds(at, PIECE_ROWS), pl.ds(q * 640, 640)]

    def send(src, dst, stage, j, target):
        copy = pltpu.make_async_remote_copy(
            src_ref=src, dst_ref=dst, send_sem=send_sems.at[stage, j],
            recv_sem=recv_sems.at[stage, j], device_id=target, device_id_type=MESH,
        )
        copy.start()
        return copy

    def add_into(dst, src, total):
        def body(i, carry):
            left = dst[i].astype(jnp.float32)
            dst[i] = (left + src[i].astype(jnp.float32)).astype(jnp.bfloat16)
            return carry

        lax.fori_loop(0, total, body, 0)

    for j, (which, cut) in enumerate(chunks):
        for half in range(2):
            for shard in range(2):
                for q in range(4):
                    pltpu.make_async_copy(
                        piece(sources[which], which, cut, shard, half, q),
                        held[j][0].at[half, shard, q], load_sems.at[j],
                    ).start()
    gain_acc[0] = gains[...]
    greet((across, core, along_y, near_z, far_z))

    partners = (core, across, along_y, near_z, far_z)
    gain_copies = []

    def gain_send(i):
        copy = pltpu.make_async_remote_copy(
            src_ref=gain_acc.at[i], dst_ref=gain_got.at[i], send_sem=gain_sems.at[0, i],
            recv_sem=gain_sems.at[1, i], device_id=partners[i], device_id_type=MESH,
        )
        copy.start()
        gain_copies.append(copy)

    def gain_step(i):
        gain_copies[i].wait_recv()
        gain_acc[i + 1] = gain_acc[i] + gain_got[i]
        if i < 4:
            gain_send(i + 1)

    copies = [[None] * count for _ in range(8)]
    gain_send(0)
    for j in range(count):
        whole = held[j][0]
        pltpu.make_async_copy(whole, whole, load_sems.at[j]).wait()
        copies[0][j] = send(whole.at[1 - c], held[j][1], 0, j, core)
    gain_step(0)
    for j in range(count):
        own, got = held[j][0], held[j][1]
        copies[0][j].wait_recv()
        add_into(own.at[c, 1 - fs], got.at[1 - fs], 4)
        copies[1][j] = send(own.at[c, 1 - fs], held[j][2], 1, j, across)
        add_into(own.at[c, fs], got.at[fs], 4)

    def stage_two(j):
        own = held[j][0]
        copies[1][j].wait_recv()
        add_into(own.at[c, fs], held[j][2], 4)
        copies[2][j] = send(
            own.at[c, fs, pl.ds(2 * (1 - y), 2)], held[j][3], 2, j, along_y
        )

    def stage_three(j):
        own = held[j][0]
        copies[2][j].wait_recv()
        add_into(own.at[c, fs, pl.ds(2 * y, 2)], held[j][3], 2)
        copies[3][j] = send(own.at[c, fs, 2 * y + 1 - z], held[j][4], 3, j, near_z)

    def stage_four(j):
        own = held[j][0]
        copies[3][j].wait_recv()
        left = own[c, fs, mine].astype(jnp.float32)
        own[c, fs, mine] = (left + held[j][4][...].astype(jnp.float32)).astype(jnp.bfloat16)
        copies[4][j] = send(own.at[c, fs, mine], held[j][5], 4, j, far_z)

    def stage_five(j):
        own, done = held[j][0], held[j][6]
        copies[4][j].wait_recv()
        left = own[c, fs, mine].astype(jnp.float32)
        done[c, mine] = (left + held[j][5][...].astype(jnp.float32)).astype(jnp.bfloat16)
        copies[5][j] = send(done.at[c, mine], done.at[c, mine], 5, j, near_z)

    def stage_six(j):
        done = held[j][6]
        copies[5][j].wait_recv()
        pair = done.at[c, pl.ds(2 * y, 2)]
        copies[6][j] = send(pair, pair, 6, j, along_y)

    def stage_seven(j):
        done = held[j][6]
        copies[6][j].wait_recv()
        copies[7][j] = send(done.at[c], done.at[c], 7, j, core)

    def stage_eight(j):
        done = held[j][6]
        which, cut = chunks[j]
        copies[7][j].wait_recv()
        for half in range(2):
            for q in range(4):
                pltpu.make_async_copy(
                    done.at[half, q], piece(sinks[which], which, cut, 0, half, q),
                    store_sems.at[j],
                ).start()

    stages = (
        stage_two, stage_three, stage_four, stage_five, stage_six, stage_seven, stage_eight,
    )
    for step in range(count + len(stages) - 1):
        for late, stage in enumerate(stages):
            j = step - late
            if 0 <= j < count:
                stage(j)
        if step < 4:
            gain_step(step + 1)
    sum_gains[...] = gain_acc[5]
    for row in copies:
        for copy in row:
            copy.wait_send()
    for copy in gain_copies:
        copy.wait_send()
    for j in range(count):
        done = held[j][6]
        pltpu.make_async_copy(done, done, store_sems.at[j]).wait()


def reduce_all(tall, wide_a, wide_b, wide_c, gains):
    def halved(full):
        return jax.ShapeDtypeStruct((full.shape[0] // 2, full.shape[1]), full.dtype)

    def scratch(cuts, width):
        tile = (PIECE_ROWS, width)
        return [
            pltpu.VMEM((cuts,) + lead + tile, jnp.bfloat16)
            for lead in ((2, 2, 4), (2, 4), (4,), (2,), (), (), (2, 4))
        ]

    anywhere = pl.BlockSpec(memory_space=pl.ANY)
    near = pl.BlockSpec(memory_space=pltpu.VMEM)
    count = TALL_CUTS + 3 * WIDE_CUTS
    return pl.pallas_call(
        reduce_kernel,
        out_shape=(
            halved(tall), halved(wide_a), halved(wide_b), halved(wide_c),
            jax.ShapeDtypeStruct(gains.shape, gains.dtype),
        ),
        in_specs=[anywhere] * 4 + [near],
        out_specs=(anywhere,) * 4 + (near,),
        scratch_shapes=scratch(TALL_CUTS, 960) + scratch(3 * WIDE_CUTS, 640) + [
            pltpu.VMEM((6,) + gains.shape, jnp.float32),
            pltpu.VMEM((5,) + gains.shape, jnp.float32),
            pltpu.SemaphoreType.DMA((count,)),
            pltpu.SemaphoreType.DMA((count,)),
            pltpu.SemaphoreType.DMA((8, count)),
            pltpu.SemaphoreType.DMA((8, count)),
            pltpu.SemaphoreType.DMA((2, 5)),
        ],
        compiler_params=pltpu.CompilerParams(
            collective_id=1, has_side_effects=True, vmem_limit_bytes=60 * 1024 * 1024
        ),
    )(tall, wide_a, wide_b, wide_c, gains)


def per_device(
    tokens,
    segments,
    cotangent,
    attn_gain,
    w_query,
    w_key,
    w_value,
    w_out,
    mlp_gain,
    w_gate,
    w_up,
    w_down,
    direct,
):
    if direct:
        attn_shard = jnp.concatenate([w_query, w_key, w_value, w_out], axis=1)
        gain_shard = jnp.pad(jnp.stack([attn_gain, mlp_gain]), ((0, 14), (0, 32)))
        attn_w, gate_w, up_w, down_w, gains = gather_all(
            attn_shard, w_gate, w_up, w_down, gain_shard
        )
        gain_one = gains[:, 0, :480].reshape(-1)
        gain_two = gains[:, 1, :480].reshape(-1)
        qkv_w, out_w = attn_w[:, :1600], attn_w[:, 1600:]
    else:
        shards = (attn_gain, w_query, w_key, w_value, w_out, mlp_gain, w_gate, w_up, w_down)
        gain_one, query_w, key_w, value_w, out_w, gain_two, gate_w, up_w, down_w = [
            lax.all_gather(shard, "fsdp", axis=0, tiled=True) for shard in shards
        ]
        qkv_w = jnp.concatenate([query_w, key_w, value_w], axis=1)
    cosine, sine = rope_tables(segments)
    resid_in = tokens.astype(jnp.float32)
    normed_one, scale_one, attn_in = norm_forward(resid_in, gain_one)
    projected = product(attn_in, qkv_w)
    queries = rotate(projected[:, :960], cosine, sine, 1.0).astype(jnp.bfloat16)
    keys = rotate(projected[:, 960:1280], cosine, sine, 1.0).astype(jnp.bfloat16)
    values = projected[:, 1280:].astype(jnp.bfloat16)
    mixed, log_totals = attend_forward(queries, keys, values, segments)
    mixed_low = mixed.astype(jnp.bfloat16)
    middle = resid_in + product(mixed_low, out_w)
    normed_two, scale_two, mlp_in = norm_forward(middle, gain_two)
    gate = product(mlp_in, gate_w)
    upward = product(mlp_in, up_w)
    sigma = jax.nn.sigmoid(gate)
    activated = (gate * sigma * upward).astype(jnp.bfloat16)
    result = middle + product(activated, down_w)
    grad_out = cotangent.astype(jnp.float32)
    grad_low = grad_out.astype(jnp.bfloat16)
    down_grad = product(activated.T, grad_low)
    grad_act = product(grad_low, down_w.T)
    grad_gate = (grad_act * upward * sigma * (1.0 + gate * (1.0 - sigma))).astype(jnp.bfloat16)
    grad_up = (grad_act * gate * sigma).astype(jnp.bfloat16)
    gate_grad = product(mlp_in.T, grad_gate)
    up_grad = product(mlp_in.T, grad_up)
    grad_mlp_in = product(grad_gate, gate_w.T) + product(grad_up, up_w.T)
    grad_norm_two, gain_two_grad = norm_backward(grad_mlp_in, normed_two, scale_two, gain_two)
    grad_middle = grad_out + grad_norm_two
    grad_middle_low = grad_middle.astype(jnp.bfloat16)
    out_grad = product(mixed_low.T, grad_middle_low)
    grad_mixed = product(grad_middle_low, out_w.T).astype(jnp.bfloat16)
    grad_queries, grad_keys, grad_values = attend_backward(
        queries, keys, values, grad_mixed, segments, log_totals
    )
    grad_query_pre = rotate(grad_queries, cosine, sine, -1.0).astype(jnp.bfloat16)
    grad_key_pre = rotate(grad_keys, cosine, sine, -1.0).astype(jnp.bfloat16)
    grad_value_pre = grad_values.astype(jnp.bfloat16)
    grad_qkv = jnp.concatenate([grad_query_pre, grad_key_pre, grad_value_pre], axis=1)
    qkv_grad = product(attn_in.T, grad_qkv)
    grad_attn_in = product(grad_qkv, qkv_w.T)
    grad_norm_one, gain_one_grad = norm_backward(grad_attn_in, normed_one, scale_one, gain_one)
    input_grad = grad_middle + grad_norm_one
    low = jnp.bfloat16
    attn_grad = jnp.concatenate([qkv_grad.astype(low), out_grad.astype(low)], axis=1)
    if direct:
        gain_rows = jnp.pad(jnp.stack([gain_one_grad, gain_two_grad]), ((0, 6), (0, 64)))
        down_sum, gate_sum, up_sum, attn_sum, gain_sum = reduce_all(
            down_grad.astype(low), gate_grad.astype(low), up_grad.astype(low), attn_grad,
            gain_rows,
        )
        at = lax.axis_index("fsdp") * 480
        gain_sums = [lax.dynamic_slice(gain_sum[i], (at,), (480,)) for i in range(2)]
    else:
        partial = (down_grad, gate_grad, up_grad, attn_grad, gain_one_grad, gain_two_grad)
        sums = []
        for grad in partial:
            share = lax.psum_scatter(
                grad.astype(low), "fsdp", scatter_dimension=0, tiled=True
            )
            sums.append(lax.psum(share, "dp"))
        down_sum, gate_sum, up_sum, attn_sum = sums[:4]
        gain_sums = sums[4:]
    totals = (
        gain_sums[0], attn_sum[:, :960], attn_sum[:, 960:1280], attn_sum[:, 1280:1600],
        attn_sum[:, 1600:], gain_sums[1], gate_sum, up_sum, down_sum,
    )
    totals = [total.astype(jnp.float32) for total in totals]
    return (result.astype(jnp.bfloat16), input_grad) + tuple(totals)


def solution(mesh):
    in_specs = (
        P(("dp", "fsdp"), None),
        P(("dp", "fsdp")),
        P(("dp", "fsdp"), None),
        P("fsdp"),
        P("fsdp", None),
        P("fsdp", None),
        P("fsdp", None),
        P("fsdp", None),
        P("fsdp"),
        P("fsdp", None),
        P("fsdp", None),
        P("fsdp", None),
    )
    out_specs = (
        P(("dp", "fsdp"), None),
        P(("dp", "fsdp"), None),
        P("fsdp"),
        P("fsdp", None),
        P("fsdp", None),
        P("fsdp", None),
        P("fsdp", None),
        P("fsdp"),
        P("fsdp", None),
        P("fsdp", None),
        P("fsdp", None),
    )
    direct = mesh.shape["dp"] == 16 and mesh.shape["fsdp"] == 2
    return jax.shard_map(
        functools.partial(per_device, direct=direct), mesh=mesh, in_specs=in_specs, out_specs=out_specs, check_vma=False
    )
```

```python
import functools

import jax
import jax.numpy as jnp
from jax import lax
from jax.experimental import pallas as pl
from jax.experimental.pallas import tpu as pltpu
from jax.sharding import PartitionSpec as P

HEADS = 15
KV_HEADS = 5
HEAD = 64


epsilon = 1e-05
rope_base = 100000.0
masked_score = -1e30


def rope_tables(segment_ids):
    places = jnp.arange(segment_ids.shape[0], dtype=jnp.int32)
    changed = jnp.concatenate([jnp.ones((1,), dtype=bool), segment_ids[1:] != segment_ids[:-1]])
    first = lax.cummax(jnp.where(changed, places, 0), axis=0)
    position = (places - first).astype(jnp.float32)
    frequency = rope_base ** (-jnp.arange(0, HEAD, 2, dtype=jnp.float32) / HEAD)
    angles = position[:, None] * frequency[None, :]
    angles = jnp.concatenate([angles, angles], axis=1)
    return (jnp.cos(angles), jnp.sin(angles))


def rotate(values, cosine, sine, direction):
    rows_total = values.shape[0]
    shaped = values.reshape(rows_total, -1, HEAD)
    midway = HEAD // 2
    turned = jnp.concatenate([-shaped[..., midway:], shaped[..., :midway]], axis=-1)
    return (shaped * cosine[:, None, :] + direction * turned * sine[:, None, :]).reshape(
        rows_total, -1
    )


def norm_forward(values, gain):
    scale_rows = lax.rsqrt(jnp.mean(values * values, axis=-1, keepdims=True) + epsilon)
    normed = values * scale_rows
    return (normed, scale_rows, (normed * gain.astype(jnp.float32)).astype(jnp.bfloat16))


def norm_backward(grad_scaled, normed, scale_rows, gain):
    gain_grad = jnp.sum(grad_scaled * normed, axis=0)
    grad_normed = grad_scaled * gain.astype(jnp.float32)
    inner = jnp.mean(grad_normed * normed, axis=-1, keepdims=True)
    return (scale_rows * (grad_normed - normed * inner), gain_grad)


def block_mask(segment_ids, first_row, last_row):
    places = jnp.arange(segment_ids.shape[0])
    same = segment_ids[first_row:last_row, None] == segment_ids[None, :last_row]
    causal = places[first_row:last_row, None] >= places[None, :last_row]
    return same & causal


def block_scores(query_block, key_block, allowed):
    scores = jnp.einsum(
        "qrd,kd->rqk", query_block, key_block, preferred_element_type=jnp.float32
    ) * HEAD ** (-0.5)
    return jnp.where(allowed[None], scores, masked_score)


def attend_forward(queries, keys, values, segment_ids):
    rows_total = queries.shape[0]
    block_rows = min(512, rows_total)
    group = HEADS // KV_HEADS
    log_totals = []
    allowed = block_mask(segment_ids, 0, block_rows)
    head_parts = []
    for kv_index in range(KV_HEADS):
        query_block = queries[0:block_rows, kv_index * group * HEAD : (kv_index + 1) * group * HEAD]
        query_block = query_block.reshape(block_rows, group, HEAD)
        key_block = keys[:block_rows, kv_index * HEAD : (kv_index + 1) * HEAD]
        value_block = values[:block_rows, kv_index * HEAD : (kv_index + 1) * HEAD]
        scores = block_scores(query_block, key_block, allowed)
        highest = jnp.max(scores, axis=-1, keepdims=True)
        exponent = jnp.exp(scores - highest)
        totals = jnp.sum(exponent, axis=-1, keepdims=True)
        probability = (exponent / totals).astype(jnp.bfloat16)
        log_totals.append(highest + jnp.log(totals))
        mixed = jnp.einsum(
            "rqk,kd->qrd", probability, value_block, preferred_element_type=jnp.float32
        )
        head_parts.append(mixed.reshape(block_rows, group * HEAD))
    mixed_rows = jnp.concatenate(head_parts, axis=1)
    return (mixed_rows, log_totals)


def attend_backward(queries, keys, values, grad_mixed, segment_ids, log_totals):
    rows_total = queries.shape[0]
    block_rows = min(512, rows_total)
    group = HEADS // KV_HEADS
    key_grads = [jnp.zeros((rows_total, HEAD), jnp.float32) for kv_index in range(KV_HEADS)]
    value_grads = [jnp.zeros((rows_total, HEAD), jnp.float32) for kv_index in range(KV_HEADS)]
    entry = 0
    allowed = block_mask(segment_ids, 0, block_rows)
    head_parts = []
    for kv_index in range(KV_HEADS):
        columns_lo = kv_index * group * HEAD
        columns_hi = (kv_index + 1) * group * HEAD
        query_block = queries[0:block_rows, columns_lo:columns_hi].reshape(block_rows, group, HEAD)
        grad_block = grad_mixed[0:block_rows, columns_lo:columns_hi].reshape(
            block_rows, group, HEAD
        )
        key_block = keys[:block_rows, kv_index * HEAD : (kv_index + 1) * HEAD]
        value_block = values[:block_rows, kv_index * HEAD : (kv_index + 1) * HEAD]
        scores = block_scores(query_block, key_block, allowed)
        probability = jnp.exp(scores - log_totals[entry])
        entry = entry + 1
        grad_prob = jnp.einsum(
            "qrd,kd->rqk", grad_block, value_block, preferred_element_type=jnp.float32
        )
        weighted = jnp.sum(probability * grad_prob, axis=-1, keepdims=True)
        grad_scores = (probability * (grad_prob - weighted)).astype(jnp.bfloat16)
        grad_query = jnp.einsum(
            "rqk,kd->qrd", grad_scores, key_block, preferred_element_type=jnp.float32
        ) * HEAD ** (-0.5)
        head_parts.append(grad_query.reshape(block_rows, group * HEAD))
        grad_key = jnp.einsum(
            "rqk,qrd->kd", grad_scores, query_block, preferred_element_type=jnp.float32
        ) * HEAD ** (-0.5)
        grad_value = jnp.einsum(
            "rqk,qrd->kd",
            probability.astype(jnp.bfloat16),
            grad_block,
            preferred_element_type=jnp.float32,
        )
        key_grads[kv_index] = grad_key
        value_grads[kv_index] = grad_value
    grad_query_rows = jnp.concatenate(head_parts, axis=1)
    return (
        grad_query_rows,
        jnp.concatenate(key_grads, axis=1),
        jnp.concatenate(value_grads, axis=1),
    )


def product(left, right):
    return jnp.dot(left, right, preferred_element_type=jnp.float32)


MESH = pl.DeviceIdType.MESH
CUTS = 3
PIECE_ROWS = 80
PIECE_COLUMNS = 640
CHUNKS = [(which, cut) for which in range(4) for cut in range(CUTS)]


def place():
    dp = lax.axis_index("dp")
    fs = lax.axis_index("fsdp")
    bits = [lax.rem(lax.div(dp, 1 << shift), 2) for shift in range(4)]
    flips = [dp + (1 << shift) - (2 << shift) * bits[shift] for shift in range(4)]
    across = (dp, 1 - fs)
    core, along_y, near_z, far_z = [(flip, fs) for flip in flips]
    return fs, bits, across, core, along_y, near_z, far_z


def greet(partners):
    barrier = pltpu.get_barrier_semaphore()
    for partner in partners:
        pl.semaphore_signal(barrier, inc=1, device_id=partner, device_id_type=MESH)
    pl.semaphore_wait(barrier, len(partners))


def aligned(value, unit):
    return pl.multiple_of(value, unit)


def piece(ref, which, cut, shard, half, q):
    if which == 3:
        rows = (cut * 4 + half * 2 + q // 2) * PIECE_ROWS
        columns = shard * 1280 + (q % 2) * PIECE_COLUMNS
    else:
        rows = shard * 480 + (cut * 2 + half) * PIECE_ROWS
        columns = q * PIECE_COLUMNS
    rows, columns = aligned(rows, 16), aligned(columns, 128)
    return ref.at[pl.ds(rows, PIECE_ROWS), pl.ds(columns, PIECE_COLUMNS)]


def gather_kernel(
    wide_a, wide_b, wide_c, turned, gains,
    full_a, full_b, full_c, full_turned, full_gains,
    held_wide, held_turned, got,
    load_sems, keep_sems, store_sems, gain_sem, send_sems, recv_sems,
):
    fs, bits, across, core, along_y, near_z, _ = place()
    c, y, z = bits[0], bits[1], bits[2]
    shards = (wide_a, wide_b, wide_c, turned)
    fulls = (full_a, full_b, full_c, full_turned)
    count = len(CHUNKS)

    def send(src, dst, stage, index, target):
        copy = pltpu.make_async_remote_copy(
            src_ref=src, dst_ref=dst, send_sem=send_sems.at[stage, index],
            recv_sem=recv_sems.at[stage, index], device_id=target, device_id_type=MESH,
        )
        copy.start()
        return copy

    loads, keeps = [], []
    for j, (which, cut) in enumerate(CHUNKS):
        if which == 3:
            held = held_turned.at[cut]
            src = turned.at[pl.ds(cut * 320, 320), :]
            dst = full_turned.at[pl.ds(cut * 320, 320), pl.ds(aligned(fs * 1280, 128), 1280)]
        else:
            held = held_wide.at[3 * which + cut]
            src = shards[which].at[pl.ds(cut * 160, 160), :]
            dst = fulls[which].at[pl.ds(aligned(fs * 480 + cut * 160, 16), 160), :]
        loads.append(pltpu.make_async_copy(src, held, load_sems.at[j]))
        keeps.append(pltpu.make_async_copy(held, dst, keep_sems.at[j]))
        loads[j].start()
    keep_gains = pltpu.make_async_copy(gains, full_gains.at[fs], gain_sem)
    keep_gains.start()
    greet((across, core, along_y, near_z))
    gain_copy = send(gains, full_gains.at[fs], 0, count, across)
    copies = [[None] * count for _ in range(4)]

    def lead(j):
        return (y, z) if j % 2 == 0 else (z, y)

    for j, (which, cut) in enumerate(CHUNKS):
        first, second = lead(j)
        loads[j].wait()
        q = 2 * first + second
        if which == 3:
            src = held_turned.at[
                cut, pl.ds(aligned((2 * c + first) * PIECE_ROWS, 16), PIECE_ROWS),
                pl.ds(aligned(second * PIECE_COLUMNS, 128), PIECE_COLUMNS),
            ]
        else:
            src = held_wide.at[
                3 * which + cut, pl.ds(aligned(c * PIECE_ROWS, 16), PIECE_ROWS),
                pl.ds(aligned(q * PIECE_COLUMNS, 128), PIECE_COLUMNS),
            ]
        copies[0][j] = send(src, got.at[j, c, q], 0, j, across)
        keeps[j].start()

    def forward_one(j):
        first, second = lead(j)
        copies[0][j].wait_recv()
        part = got.at[j, c, 2 * first + second]
        copies[1][j] = send(part, part, 1, j, near_z if j % 2 == 0 else along_y)

    def forward_two(j):
        first, _ = lead(j)
        copies[1][j].wait_recv()
        part = got.at[j, c, pl.ds(2 * first, 2)]
        copies[2][j] = send(part, part, 2, j, along_y if j % 2 == 0 else near_z)

    def forward_four(j):
        copies[2][j].wait_recv()
        copies[3][j] = send(got.at[j, c], got.at[j, c], 3, j, core)

    def store(j):
        which, cut = CHUNKS[j]
        copies[3][j].wait_recv()
        for half in range(2):
            for q in range(4):
                pltpu.make_async_copy(
                    got.at[j, half, q], piece(fulls[which], which, cut, 1 - fs, half, q),
                    store_sems.at[j],
                ).start()

    stages = (forward_one, forward_two, forward_four, store)
    for step in range(count + len(stages) - 1):
        for late, stage in enumerate(stages):
            if 0 <= step - late < count:
                stage(step - late)
    gain_copy.wait()
    keep_gains.wait()
    for j in range(count):
        keeps[j].wait()
        pltpu.make_async_copy(got.at[j], got.at[j], store_sems.at[j]).wait()
    for row in copies:
        for copy in row:
            copy.wait_send()


def gather_all(wide_a, wide_b, wide_c, turned, gains):
    full = jax.ShapeDtypeStruct((960, 2560), jnp.bfloat16)
    anywhere = pl.BlockSpec(memory_space=pl.ANY)
    count = len(CHUNKS)
    return pl.pallas_call(
        gather_kernel,
        out_shape=(full,) * 4 + (jax.ShapeDtypeStruct((2,) + gains.shape, gains.dtype),),
        in_specs=[anywhere] * 5,
        out_specs=(anywhere,) * 5,
        scratch_shapes=[
            pltpu.VMEM((9, 160, 2560), jnp.bfloat16),
            pltpu.VMEM((3, 320, 1280), jnp.bfloat16),
            pltpu.VMEM((count, 2, 4, PIECE_ROWS, PIECE_COLUMNS), jnp.bfloat16),
            pltpu.SemaphoreType.DMA((count,)),
            pltpu.SemaphoreType.DMA((count,)),
            pltpu.SemaphoreType.DMA((count,)),
            pltpu.SemaphoreType.DMA,
            pltpu.SemaphoreType.DMA((4, count + 1)),
            pltpu.SemaphoreType.DMA((4, count + 1)),
        ],
        compiler_params=pltpu.CompilerParams(
            collective_id=0, has_side_effects=True, vmem_limit_bytes=40 * 1024 * 1024
        ),
    )(wide_a, wide_b, wide_c, turned, gains)


def reduce_kernel(
    wide_a, wide_b, wide_c, turned, gains,
    sum_a, sum_b, sum_c, sum_turned, sum_gains,
    own_all, core_all, across_all, y_all, near_all, far_all, done_all,
    gain_acc, gain_got, load_sems, store_sems, send_sems, recv_sems, gain_sems,
):
    fs, bits, across, core, along_y, near_z, far_z = place()
    c, y, z = bits[0], bits[1], bits[2]
    mine = 2 * y + z
    sources = (wide_a, wide_b, wide_c, turned)
    sinks = (sum_a, sum_b, sum_c, sum_turned)
    chunks = CHUNKS[::-1]
    count = len(chunks)
    scratches = (own_all, core_all, across_all, y_all, near_all, far_all, done_all)
    held = [[ref.at[j] for ref in scratches] for j in range(count)]

    def send(src, dst, stage, j, target):
        copy = pltpu.make_async_remote_copy(
            src_ref=src, dst_ref=dst, send_sem=send_sems.at[stage, j],
            recv_sem=recv_sems.at[stage, j], device_id=target, device_id_type=MESH,
        )
        copy.start()
        return copy

    def add_into(dst, src, total):
        def body(i, carry):
            left = dst[i].astype(jnp.float32)
            dst[i] = (left + src[i].astype(jnp.float32)).astype(jnp.bfloat16)
            return carry

        lax.fori_loop(0, total, body, 0)

    for j, (which, cut) in enumerate(chunks):
        for half in range(2):
            for shard in range(2):
                for q in range(4):
                    pltpu.make_async_copy(
                        piece(sources[which], which, cut, shard, half, q),
                        held[j][0].at[half, shard, q], load_sems.at[j],
                    ).start()
    gain_acc[0] = gains[...]
    greet((across, core, along_y, near_z, far_z))

    partners = (core, across, along_y, near_z, far_z)
    gain_copies = []

    def gain_send(i):
        copy = pltpu.make_async_remote_copy(
            src_ref=gain_acc.at[i], dst_ref=gain_got.at[i], send_sem=gain_sems.at[0, i],
            recv_sem=gain_sems.at[1, i], device_id=partners[i], device_id_type=MESH,
        )
        copy.start()
        gain_copies.append(copy)

    def gain_step(i):
        gain_copies[i].wait_recv()
        gain_acc[i + 1] = gain_acc[i] + gain_got[i]
        if i < 4:
            gain_send(i + 1)

    copies = [[None] * count for _ in range(8)]
    gain_send(0)
    for j in range(count):
        whole = held[j][0]
        pltpu.make_async_copy(whole, whole, load_sems.at[j]).wait()
        copies[0][j] = send(whole.at[1 - c], held[j][1], 0, j, core)
    gain_step(0)
    for j in range(count):
        own, got = held[j][0], held[j][1]
        copies[0][j].wait_recv()
        add_into(own.at[c, 1 - fs], got.at[1 - fs], 4)
        copies[1][j] = send(own.at[c, 1 - fs], held[j][2], 1, j, across)
        add_into(own.at[c, fs], got.at[fs], 4)

    def stage_two(j):
        own = held[j][0]
        copies[1][j].wait_recv()
        add_into(own.at[c, fs], held[j][2], 4)
        copies[2][j] = send(
            own.at[c, fs, pl.ds(2 * (1 - y), 2)], held[j][3], 2, j, along_y
        )

    def stage_three(j):
        own = held[j][0]
        copies[2][j].wait_recv()
        add_into(own.at[c, fs, pl.ds(2 * y, 2)], held[j][3], 2)
        copies[3][j] = send(own.at[c, fs, 2 * y + 1 - z], held[j][4], 3, j, near_z)

    def stage_four(j):
        own = held[j][0]
        copies[3][j].wait_recv()
        left = own[c, fs, mine].astype(jnp.float32)
        own[c, fs, mine] = (left + held[j][4][...].astype(jnp.float32)).astype(jnp.bfloat16)
        copies[4][j] = send(own.at[c, fs, mine], held[j][5], 4, j, far_z)

    def stage_five(j):
        own, done = held[j][0], held[j][6]
        copies[4][j].wait_recv()
        left = own[c, fs, mine].astype(jnp.float32)
        done[c, mine] = (left + held[j][5][...].astype(jnp.float32)).astype(jnp.bfloat16)
        copies[5][j] = send(done.at[c, mine], done.at[c, mine], 5, j, near_z)

    def stage_six(j):
        done = held[j][6]
        copies[5][j].wait_recv()
        pair = done.at[c, pl.ds(2 * y, 2)]
        copies[6][j] = send(pair, pair, 6, j, along_y)

    def stage_seven(j):
        done = held[j][6]
        copies[6][j].wait_recv()
        copies[7][j] = send(done.at[c], done.at[c], 7, j, core)

    def stage_eight(j):
        done = held[j][6]
        which, cut = chunks[j]
        copies[7][j].wait_recv()
        for half in range(2):
            for q in range(4):
                pltpu.make_async_copy(
                    done.at[half, q], piece(sinks[which], which, cut, 0, half, q),
                    store_sems.at[j],
                ).start()

    stages = (
        stage_two, stage_three, stage_four, stage_five, stage_six, stage_seven, stage_eight,
    )
    for step in range(count + len(stages) - 1):
        for late, stage in enumerate(stages):
            j = step - late
            if 0 <= j < count:
                stage(j)
        if step < 4:
            gain_step(step + 1)
    sum_gains[...] = gain_acc[5]
    for row in copies:
        for copy in row:
            copy.wait_send()
    for copy in gain_copies:
        copy.wait_send()
    for j in range(count):
        done = held[j][6]
        pltpu.make_async_copy(done, done, store_sems.at[j]).wait()


def reduce_all(wide_a, wide_b, wide_c, turned, gains):
    half = jax.ShapeDtypeStruct((480, 2560), jnp.bfloat16)
    half_turned = jax.ShapeDtypeStruct((960, 1280), jnp.bfloat16)
    count = len(CHUNKS)
    anywhere = pl.BlockSpec(memory_space=pl.ANY)
    near = pl.BlockSpec(memory_space=pltpu.VMEM)
    return pl.pallas_call(
        reduce_kernel,
        out_shape=(
            half, half, half, half_turned, jax.ShapeDtypeStruct(gains.shape, gains.dtype),
        ),
        in_specs=[anywhere] * 4 + [near],
        out_specs=(anywhere,) * 4 + (near,),
        scratch_shapes=[
            pltpu.VMEM((count,) + lead + (PIECE_ROWS, PIECE_COLUMNS), jnp.bfloat16)
            for lead in ((2, 2, 4), (2, 4), (4,), (2,), (), (), (2, 4))
        ] + [
            pltpu.VMEM((6,) + gains.shape, jnp.float32),
            pltpu.VMEM((5,) + gains.shape, jnp.float32),
            pltpu.SemaphoreType.DMA((count,)),
            pltpu.SemaphoreType.DMA((count,)),
            pltpu.SemaphoreType.DMA((8, count)),
            pltpu.SemaphoreType.DMA((8, count)),
            pltpu.SemaphoreType.DMA((2, 5)),
        ],
        compiler_params=pltpu.CompilerParams(
            collective_id=1, has_side_effects=True, vmem_limit_bytes=60 * 1024 * 1024
        ),
    )(wide_a, wide_b, wide_c, turned, gains)


def per_device(
    tokens,
    segments,
    cotangent,
    attn_gain,
    w_query,
    w_key,
    w_value,
    w_out,
    mlp_gain,
    w_gate,
    w_up,
    w_down,
    direct,
):
    if direct:
        attn_shard = jnp.concatenate([w_query, w_key, w_value, w_out], axis=1)
        gain_shard = jnp.pad(jnp.stack([attn_gain, mlp_gain]), ((0, 14), (0, 32)))
        attn_w, gate_w, up_w, down_turned, gains = gather_all(
            attn_shard, w_gate, w_up, w_down.T, gain_shard
        )
        gain_one = gains[:, 0, :480].reshape(-1)
        gain_two = gains[:, 1, :480].reshape(-1)
        qkv_w, out_w = attn_w[:, :1600], attn_w[:, 1600:]
    else:
        shards = (attn_gain, w_query, w_key, w_value, w_out, mlp_gain, w_gate, w_up, w_down)
        gain_one, query_w, key_w, value_w, out_w, gain_two, gate_w, up_w, down_w = [
            lax.all_gather(shard, "fsdp", axis=0, tiled=True) for shard in shards
        ]
        qkv_w = jnp.concatenate([query_w, key_w, value_w], axis=1)
        down_turned = down_w.T
    cosine, sine = rope_tables(segments)
    resid_in = tokens.astype(jnp.float32)
    normed_one, scale_one, attn_in = norm_forward(resid_in, gain_one)
    projected = product(attn_in, qkv_w)
    queries = rotate(projected[:, :960], cosine, sine, 1.0).astype(jnp.bfloat16)
    keys = rotate(projected[:, 960:1280], cosine, sine, 1.0).astype(jnp.bfloat16)
    values = projected[:, 1280:].astype(jnp.bfloat16)
    mixed, log_totals = attend_forward(queries, keys, values, segments)
    mixed_low = mixed.astype(jnp.bfloat16)
    middle = resid_in + product(mixed_low, out_w)
    normed_two, scale_two, mlp_in = norm_forward(middle, gain_two)
    gate = product(mlp_in, gate_w)
    upward = product(mlp_in, up_w)
    sigma = jax.nn.sigmoid(gate)
    activated = (gate * sigma * upward).astype(jnp.bfloat16)
    result = middle + product(activated, down_turned.T)
    grad_out = cotangent.astype(jnp.float32)
    grad_low = grad_out.astype(jnp.bfloat16)
    down_grad = product(grad_low.T, activated)
    grad_act = product(grad_low, down_turned)
    grad_gate = (grad_act * upward * sigma * (1.0 + gate * (1.0 - sigma))).astype(jnp.bfloat16)
    grad_up = (grad_act * gate * sigma).astype(jnp.bfloat16)
    gate_grad = product(mlp_in.T, grad_gate)
    up_grad = product(mlp_in.T, grad_up)
    grad_mlp_in = product(grad_gate, gate_w.T) + product(grad_up, up_w.T)
    grad_norm_two, gain_two_grad = norm_backward(grad_mlp_in, normed_two, scale_two, gain_two)
    grad_middle = grad_out + grad_norm_two
    grad_middle_low = grad_middle.astype(jnp.bfloat16)
    out_grad = product(mixed_low.T, grad_middle_low)
    grad_mixed = product(grad_middle_low, out_w.T).astype(jnp.bfloat16)
    grad_queries, grad_keys, grad_values = attend_backward(
        queries, keys, values, grad_mixed, segments, log_totals
    )
    grad_query_pre = rotate(grad_queries, cosine, sine, -1.0).astype(jnp.bfloat16)
    grad_key_pre = rotate(grad_keys, cosine, sine, -1.0).astype(jnp.bfloat16)
    grad_value_pre = grad_values.astype(jnp.bfloat16)
    grad_qkv = jnp.concatenate([grad_query_pre, grad_key_pre, grad_value_pre], axis=1)
    qkv_grad = product(attn_in.T, grad_qkv)
    grad_attn_in = product(grad_qkv, qkv_w.T)
    grad_norm_one, gain_one_grad = norm_backward(grad_attn_in, normed_one, scale_one, gain_one)
    input_grad = grad_middle + grad_norm_one
    low = jnp.bfloat16
    attn_grad = jnp.concatenate([qkv_grad.astype(low), out_grad.astype(low)], axis=1)
    if direct:
        gain_rows = jnp.pad(jnp.stack([gain_one_grad, gain_two_grad]), ((0, 6), (0, 64)))
        attn_sum, gate_sum, up_sum, down_sum, gain_sum = reduce_all(
            attn_grad, gate_grad.astype(low), up_grad.astype(low), down_grad.astype(low),
            gain_rows,
        )
        down_sum = down_sum.T
        at = lax.axis_index("fsdp") * 480
        gain_sums = [lax.dynamic_slice(gain_sum[i], (at,), (480,)) for i in range(2)]
    else:
        partial = (down_grad.T, gate_grad, up_grad, attn_grad, gain_one_grad, gain_two_grad)
        sums = []
        for grad in partial:
            share = lax.psum_scatter(
                grad.astype(low), "fsdp", scatter_dimension=0, tiled=True
            )
            sums.append(lax.psum(share, "dp"))
        down_sum, gate_sum, up_sum, attn_sum = sums[:4]
        gain_sums = sums[4:]
    totals = (
        gain_sums[0], attn_sum[:, :960], attn_sum[:, 960:1280], attn_sum[:, 1280:1600],
        attn_sum[:, 1600:], gain_sums[1], gate_sum, up_sum, down_sum,
    )
    totals = [total.astype(jnp.float32) for total in totals]
    return (result.astype(jnp.bfloat16), input_grad) + tuple(totals)


def solution(mesh):
    in_specs = (
        P(("dp", "fsdp"), None),
        P(("dp", "fsdp")),
        P(("dp", "fsdp"), None),
        P("fsdp"),
        P("fsdp", None),
        P("fsdp", None),
        P("fsdp", None),
        P("fsdp", None),
        P("fsdp"),
        P("fsdp", None),
        P("fsdp", None),
        P("fsdp", None),
    )
    out_specs = (
        P(("dp", "fsdp"), None),
        P(("dp", "fsdp"), None),
        P("fsdp"),
        P("fsdp", None),
        P("fsdp", None),
        P("fsdp", None),
        P("fsdp", None),
        P("fsdp"),
        P("fsdp", None),
        P("fsdp", None),
        P("fsdp", None),
    )
    direct = mesh.shape["dp"] == 16 and mesh.shape["fsdp"] == 2
    return jax.shard_map(
        functools.partial(per_device, direct=direct), mesh=mesh, in_specs=in_specs, out_specs=out_specs, check_vma=False
    )
```

```python
import functools

import jax
import jax.numpy as jnp
from jax import lax
from jax.experimental import pallas as pl
from jax.experimental.pallas import tpu as pltpu
from jax.sharding import PartitionSpec as P

HEADS = 15
KV_HEADS = 5
HEAD = 64


epsilon = 1e-05
rope_base = 100000.0
masked_score = -1e30


def rope_tables(segment_ids):
    places = jnp.arange(segment_ids.shape[0], dtype=jnp.int32)
    changed = jnp.concatenate([jnp.ones((1,), dtype=bool), segment_ids[1:] != segment_ids[:-1]])
    first = lax.cummax(jnp.where(changed, places, 0), axis=0)
    position = (places - first).astype(jnp.float32)
    frequency = rope_base ** (-jnp.arange(0, HEAD, 2, dtype=jnp.float32) / HEAD)
    angles = position[:, None] * frequency[None, :]
    angles = jnp.concatenate([angles, angles], axis=1)
    return (jnp.cos(angles), jnp.sin(angles))


def rotate(values, cosine, sine, direction):
    rows_total = values.shape[0]
    shaped = values.reshape(rows_total, -1, HEAD)
    midway = HEAD // 2
    turned = jnp.concatenate([-shaped[..., midway:], shaped[..., :midway]], axis=-1)
    return (shaped * cosine[:, None, :] + direction * turned * sine[:, None, :]).reshape(
        rows_total, -1
    )


def norm_forward(values, gain):
    scale_rows = lax.rsqrt(jnp.mean(values * values, axis=-1, keepdims=True) + epsilon)
    normed = values * scale_rows
    return (normed, scale_rows, (normed * gain.astype(jnp.float32)).astype(jnp.bfloat16))


def norm_backward(grad_scaled, normed, scale_rows, gain):
    gain_grad = jnp.sum(grad_scaled * normed, axis=0)
    grad_normed = grad_scaled * gain.astype(jnp.float32)
    inner = jnp.mean(grad_normed * normed, axis=-1, keepdims=True)
    return (scale_rows * (grad_normed - normed * inner), gain_grad)


def block_mask(segment_ids, first_row, last_row):
    places = jnp.arange(segment_ids.shape[0])
    same = segment_ids[first_row:last_row, None] == segment_ids[None, :last_row]
    causal = places[first_row:last_row, None] >= places[None, :last_row]
    return same & causal


def block_scores(query_block, key_block, allowed):
    scores = jnp.einsum(
        "qrd,kd->rqk", query_block, key_block, preferred_element_type=jnp.float32
    ) * HEAD ** (-0.5)
    return jnp.where(allowed[None], scores, masked_score)


def attend_forward(queries, keys, values, segment_ids):
    rows_total = queries.shape[0]
    block_rows = min(512, rows_total)
    group = HEADS // KV_HEADS
    log_totals = []
    allowed = block_mask(segment_ids, 0, block_rows)
    head_parts = []
    for kv_index in range(KV_HEADS):
        query_block = queries[0:block_rows, kv_index * group * HEAD : (kv_index + 1) * group * HEAD]
        query_block = query_block.reshape(block_rows, group, HEAD)
        key_block = keys[:block_rows, kv_index * HEAD : (kv_index + 1) * HEAD]
        value_block = values[:block_rows, kv_index * HEAD : (kv_index + 1) * HEAD]
        scores = block_scores(query_block, key_block, allowed)
        highest = jnp.max(scores, axis=-1, keepdims=True)
        exponent = jnp.exp(scores - highest)
        totals = jnp.sum(exponent, axis=-1, keepdims=True)
        probability = (exponent / totals).astype(jnp.bfloat16)
        log_totals.append(highest + jnp.log(totals))
        mixed = jnp.einsum(
            "rqk,kd->qrd", probability, value_block, preferred_element_type=jnp.float32
        )
        head_parts.append(mixed.reshape(block_rows, group * HEAD))
    mixed_rows = jnp.concatenate(head_parts, axis=1)
    return (mixed_rows, log_totals)


def attend_backward(queries, keys, values, grad_mixed, segment_ids, log_totals):
    rows_total = queries.shape[0]
    block_rows = min(512, rows_total)
    group = HEADS // KV_HEADS
    key_grads = [jnp.zeros((rows_total, HEAD), jnp.float32) for kv_index in range(KV_HEADS)]
    value_grads = [jnp.zeros((rows_total, HEAD), jnp.float32) for kv_index in range(KV_HEADS)]
    entry = 0
    allowed = block_mask(segment_ids, 0, block_rows)
    head_parts = []
    for kv_index in range(KV_HEADS):
        columns_lo = kv_index * group * HEAD
        columns_hi = (kv_index + 1) * group * HEAD
        query_block = queries[0:block_rows, columns_lo:columns_hi].reshape(block_rows, group, HEAD)
        grad_block = grad_mixed[0:block_rows, columns_lo:columns_hi].reshape(
            block_rows, group, HEAD
        )
        key_block = keys[:block_rows, kv_index * HEAD : (kv_index + 1) * HEAD]
        value_block = values[:block_rows, kv_index * HEAD : (kv_index + 1) * HEAD]
        scores = block_scores(query_block, key_block, allowed)
        probability = jnp.exp(scores - log_totals[entry])
        entry = entry + 1
        grad_prob = jnp.einsum(
            "qrd,kd->rqk", grad_block, value_block, preferred_element_type=jnp.float32
        )
        weighted = jnp.sum(probability * grad_prob, axis=-1, keepdims=True)
        grad_scores = (probability * (grad_prob - weighted)).astype(jnp.bfloat16)
        grad_query = jnp.einsum(
            "rqk,kd->qrd", grad_scores, key_block, preferred_element_type=jnp.float32
        ) * HEAD ** (-0.5)
        head_parts.append(grad_query.reshape(block_rows, group * HEAD))
        grad_key = jnp.einsum(
            "rqk,qrd->kd", grad_scores, query_block, preferred_element_type=jnp.float32
        ) * HEAD ** (-0.5)
        grad_value = jnp.einsum(
            "rqk,qrd->kd",
            probability.astype(jnp.bfloat16),
            grad_block,
            preferred_element_type=jnp.float32,
        )
        key_grads[kv_index] = grad_key
        value_grads[kv_index] = grad_value
    grad_query_rows = jnp.concatenate(head_parts, axis=1)
    return (
        grad_query_rows,
        jnp.concatenate(key_grads, axis=1),
        jnp.concatenate(value_grads, axis=1),
    )


def product(left, right):
    return jnp.dot(left, right, preferred_element_type=jnp.float32)


MESH = pl.DeviceIdType.MESH
CUTS = 3
PIECE_ROWS = 80
PIECE_COLUMNS = 640
CHUNKS = [(which, cut) for which in range(4) for cut in range(CUTS)]


def place():
    dp = lax.axis_index("dp")
    fs = lax.axis_index("fsdp")
    bits = [lax.rem(lax.div(dp, 1 << shift), 2) for shift in range(4)]
    flips = [dp + (1 << shift) - (2 << shift) * bits[shift] for shift in range(4)]
    across = (dp, 1 - fs)
    core, along_y, near_z, far_z = [(flip, fs) for flip in flips]
    return fs, bits, across, core, along_y, near_z, far_z


def greet(partners):
    barrier = pltpu.get_barrier_semaphore()
    for partner in partners:
        pl.semaphore_signal(barrier, inc=1, device_id=partner, device_id_type=MESH)
    pl.semaphore_wait(barrier, len(partners))


def aligned(value, unit):
    return pl.multiple_of(value, unit)


def piece(ref, which, cut, shard, half, q):
    if which == 3:
        rows = (cut * 4 + half * 2 + q // 2) * PIECE_ROWS
        columns = shard * 1280 + (q % 2) * PIECE_COLUMNS
    else:
        rows = shard * 480 + (cut * 2 + half) * PIECE_ROWS
        columns = q * PIECE_COLUMNS
    rows, columns = aligned(rows, 16), aligned(columns, 128)
    return ref.at[pl.ds(rows, PIECE_ROWS), pl.ds(columns, PIECE_COLUMNS)]


def gather_kernel(
    wide_a, wide_b, wide_c, turned, gains,
    full_a, full_b, full_c, full_turned, full_gains,
    held_wide, held_turned, got,
    load_sems, keep_sems, store_sems, gain_sem, send_sems, recv_sems,
):
    fs, bits, across, core, along_y, near_z, _ = place()
    c, y, z = bits[0], bits[1], bits[2]
    shards = (wide_a, wide_b, wide_c, turned)
    fulls = (full_a, full_b, full_c, full_turned)
    count = len(CHUNKS)

    def send(src, dst, stage, index, target):
        copy = pltpu.make_async_remote_copy(
            src_ref=src, dst_ref=dst, send_sem=send_sems.at[stage, index],
            recv_sem=recv_sems.at[stage, index], device_id=target, device_id_type=MESH,
        )
        copy.start()
        return copy

    loads, keeps = [], []
    for j, (which, cut) in enumerate(CHUNKS):
        if which == 3:
            held = held_turned.at[cut]
            src = turned.at[pl.ds(cut * 320, 320), :]
            dst = full_turned.at[pl.ds(cut * 320, 320), pl.ds(aligned(fs * 1280, 128), 1280)]
        else:
            held = held_wide.at[3 * which + cut]
            src = shards[which].at[pl.ds(cut * 160, 160), :]
            dst = fulls[which].at[pl.ds(aligned(fs * 480 + cut * 160, 16), 160), :]
        loads.append(pltpu.make_async_copy(src, held, load_sems.at[j]))
        keeps.append(pltpu.make_async_copy(held, dst, keep_sems.at[j]))
        loads[j].start()
    keep_gains = pltpu.make_async_copy(gains, full_gains.at[fs], gain_sem)
    keep_gains.start()
    greet((across, core, along_y, near_z))
    gain_copy = send(gains, full_gains.at[fs], 0, count, across)
    copies = [[None] * count for _ in range(4)]

    def lead(j):
        return (y, z) if j % 2 == 0 else (z, y)

    for j, (which, cut) in enumerate(CHUNKS):
        first, second = lead(j)
        loads[j].wait()
        q = 2 * first + second
        if which == 3:
            src = held_turned.at[
                cut, pl.ds(aligned((2 * c + first) * PIECE_ROWS, 16), PIECE_ROWS),
                pl.ds(aligned(second * PIECE_COLUMNS, 128), PIECE_COLUMNS),
            ]
        else:
            src = held_wide.at[
                3 * which + cut, pl.ds(aligned(c * PIECE_ROWS, 16), PIECE_ROWS),
                pl.ds(aligned(q * PIECE_COLUMNS, 128), PIECE_COLUMNS),
            ]
        copies[0][j] = send(src, got.at[j, c, q], 0, j, across)
        keeps[j].start()

    def forward_one(j):
        first, second = lead(j)
        copies[0][j].wait_recv()
        part = got.at[j, c, 2 * first + second]
        copies[1][j] = send(part, part, 1, j, near_z if j % 2 == 0 else along_y)

    def forward_two(j):
        first, _ = lead(j)
        copies[1][j].wait_recv()
        part = got.at[j, c, pl.ds(2 * first, 2)]
        copies[2][j] = send(part, part, 2, j, along_y if j % 2 == 0 else near_z)

    def forward_four(j):
        copies[2][j].wait_recv()
        copies[3][j] = send(got.at[j, c], got.at[j, c], 3, j, core)

    def store(j):
        which, cut = CHUNKS[j]
        copies[3][j].wait_recv()
        for half in range(2):
            for q in range(4):
                pltpu.make_async_copy(
                    got.at[j, half, q], piece(fulls[which], which, cut, 1 - fs, half, q),
                    store_sems.at[j],
                ).start()

    stages = (forward_one, forward_two, forward_four, store)
    for step in range(count + len(stages) - 1):
        for late, stage in enumerate(stages):
            if 0 <= step - late < count:
                stage(step - late)
    gain_copy.wait()
    keep_gains.wait()
    for j in range(count):
        keeps[j].wait()
        pltpu.make_async_copy(got.at[j], got.at[j], store_sems.at[j]).wait()
    for row in copies:
        for copy in row:
            copy.wait_send()


def gather_all(wide_a, wide_b, wide_c, turned, gains):
    full = jax.ShapeDtypeStruct((960, 2560), jnp.bfloat16)
    anywhere = pl.BlockSpec(memory_space=pl.ANY)
    count = len(CHUNKS)
    return pl.pallas_call(
        gather_kernel,
        out_shape=(full,) * 4 + (jax.ShapeDtypeStruct((2,) + gains.shape, gains.dtype),),
        in_specs=[anywhere] * 5,
        out_specs=(anywhere,) * 5,
        scratch_shapes=[
            pltpu.VMEM((9, 160, 2560), jnp.bfloat16),
            pltpu.VMEM((3, 320, 1280), jnp.bfloat16),
            pltpu.VMEM((count, 2, 4, PIECE_ROWS, PIECE_COLUMNS), jnp.bfloat16),
            pltpu.SemaphoreType.DMA((count,)),
            pltpu.SemaphoreType.DMA((count,)),
            pltpu.SemaphoreType.DMA((count,)),
            pltpu.SemaphoreType.DMA,
            pltpu.SemaphoreType.DMA((4, count + 1)),
            pltpu.SemaphoreType.DMA((4, count + 1)),
        ],
        compiler_params=pltpu.CompilerParams(
            collective_id=0, has_side_effects=True, vmem_limit_bytes=40 * 1024 * 1024
        ),
    )(wide_a, wide_b, wide_c, turned, gains)


def reduce_kernel(
    wide_a, mlp_turned, gate_right, up_right, out_turned, act_right, gains,
    sum_a, sum_b, sum_c, sum_turned, sum_gains,
    own_all, core_all, across_all, y_all, near_all, far_all, done_all,
    gain_acc, gain_got, load_sems, store_sems, send_sems, recv_sems, gain_sems,
):
    fs, bits, across, core, along_y, near_z, far_z = place()
    c, y, z = bits[0], bits[1], bits[2]
    mine = 2 * y + z
    lefts = (None, mlp_turned, mlp_turned, out_turned)
    rights = (None, gate_right, up_right, act_right)
    sinks = (sum_a, sum_b, sum_c, sum_turned)
    chunks = CHUNKS[::-1]
    count = len(chunks)
    scratches = (own_all, core_all, across_all, y_all, near_all, far_all, done_all)
    held = [[ref.at[j] for ref in scratches] for j in range(count)]

    def send(src, dst, stage, j, target):
        copy = pltpu.make_async_remote_copy(
            src_ref=src, dst_ref=dst, send_sem=send_sems.at[stage, j],
            recv_sem=recv_sems.at[stage, j], device_id=target, device_id_type=MESH,
        )
        copy.start()
        return copy

    def add_into(dst, src, total):
        def body(i, carry):
            left = dst[i].astype(jnp.float32)
            dst[i] = (left + src[i].astype(jnp.float32)).astype(jnp.bfloat16)
            return carry

        lax.fori_loop(0, total, body, 0)

    def load(j):
        cut = chunks[j][1]
        for half in range(2):
            for shard in range(2):
                for q in range(4):
                    pltpu.make_async_copy(
                        piece(wide_a, 0, cut, shard, half, q),
                        held[j][0].at[half, shard, q], load_sems.at[j],
                    ).start()

    def weight_grad(j):
        which, cut = chunks[j]
        left, right, own = lefts[which], rights[which], held[j][0]

        def block(b, carry):
            columns = right[:, pl.ds(pl.multiple_of(b * PIECE_COLUMNS, 128), PIECE_COLUMNS)]
            if which == 3:
                got = product(left[cut * 320 : (cut + 1) * 320, :], columns)
                got = got.astype(jnp.bfloat16)
                for half in range(2):
                    for r in range(2):
                        at = (half * 2 + r) * PIECE_ROWS
                        own[half, lax.div(b, 2), 2 * r + lax.rem(b, 2)] = got[at : at + PIECE_ROWS]
            else:
                for shard in range(2):
                    at = shard * 480 + cut * 160
                    got = product(left[at : at + 160, :], columns).astype(jnp.bfloat16)
                    own[0, shard, b] = got[:PIECE_ROWS]
                    own[1, shard, b] = got[PIECE_ROWS:]
            return carry

        lax.fori_loop(0, 4, block, 0)

    for j, (which, cut) in enumerate(chunks):
        if which == 0:
            load(j)
    gain_acc[0] = gains[...]
    greet((across, core, along_y, near_z, far_z))

    partners = (core, across, along_y, near_z, far_z)
    gain_copies = []

    def gain_send(i):
        copy = pltpu.make_async_remote_copy(
            src_ref=gain_acc.at[i], dst_ref=gain_got.at[i], send_sem=gain_sems.at[0, i],
            recv_sem=gain_sems.at[1, i], device_id=partners[i], device_id_type=MESH,
        )
        copy.start()
        gain_copies.append(copy)

    def gain_step(i):
        gain_copies[i].wait_recv()
        gain_acc[i + 1] = gain_acc[i] + gain_got[i]
        if i < 4:
            gain_send(i + 1)

    copies = [[None] * count for _ in range(8)]
    gain_send(0)
    def stage_zero(j):
        whole = held[j][0]
        if chunks[j][0] == 0:
            pltpu.make_async_copy(whole, whole, load_sems.at[j]).wait()
        else:
            weight_grad(j)
        copies[0][j] = send(whole.at[1 - c], held[j][1], 0, j, core)

    def stage_one(j):
        own, got = held[j][0], held[j][1]
        copies[0][j].wait_recv()
        add_into(own.at[c, 1 - fs], got.at[1 - fs], 4)
        copies[1][j] = send(own.at[c, 1 - fs], held[j][2], 1, j, across)
        add_into(own.at[c, fs], got.at[fs], 4)

    for step in range(count + 1):
        if step < count:
            stage_zero(step)
        if step >= 1:
            stage_one(step - 1)
    gain_step(0)

    def stage_two(j):
        own = held[j][0]
        copies[1][j].wait_recv()
        add_into(own.at[c, fs], held[j][2], 4)
        copies[2][j] = send(
            own.at[c, fs, pl.ds(2 * (1 - y), 2)], held[j][3], 2, j, along_y
        )

    def stage_three(j):
        own = held[j][0]
        copies[2][j].wait_recv()
        add_into(own.at[c, fs, pl.ds(2 * y, 2)], held[j][3], 2)
        copies[3][j] = send(own.at[c, fs, 2 * y + 1 - z], held[j][4], 3, j, near_z)

    def stage_four(j):
        own = held[j][0]
        copies[3][j].wait_recv()
        left = own[c, fs, mine].astype(jnp.float32)
        own[c, fs, mine] = (left + held[j][4][...].astype(jnp.float32)).astype(jnp.bfloat16)
        copies[4][j] = send(own.at[c, fs, mine], held[j][5], 4, j, far_z)

    def stage_five(j):
        own, done = held[j][0], held[j][6]
        copies[4][j].wait_recv()
        left = own[c, fs, mine].astype(jnp.float32)
        done[c, mine] = (left + held[j][5][...].astype(jnp.float32)).astype(jnp.bfloat16)
        copies[5][j] = send(done.at[c, mine], done.at[c, mine], 5, j, near_z)

    def stage_six(j):
        done = held[j][6]
        copies[5][j].wait_recv()
        pair = done.at[c, pl.ds(2 * y, 2)]
        copies[6][j] = send(pair, pair, 6, j, along_y)

    def stage_seven(j):
        done = held[j][6]
        copies[6][j].wait_recv()
        copies[7][j] = send(done.at[c], done.at[c], 7, j, core)

    def stage_eight(j):
        done = held[j][6]
        which, cut = chunks[j]
        copies[7][j].wait_recv()
        for half in range(2):
            for q in range(4):
                pltpu.make_async_copy(
                    done.at[half, q], piece(sinks[which], which, cut, 0, half, q),
                    store_sems.at[j],
                ).start()

    stages = (
        stage_two, stage_three, stage_four, stage_five, stage_six, stage_seven, stage_eight,
    )
    for step in range(count + len(stages) - 1):
        for late, stage in enumerate(stages):
            j = step - late
            if 0 <= j < count:
                stage(j)
        if step < 4:
            gain_step(step + 1)
    sum_gains[...] = gain_acc[5]
    for row in copies:
        for copy in row:
            copy.wait_send()
    for copy in gain_copies:
        copy.wait_send()
    for j in range(count):
        done = held[j][6]
        pltpu.make_async_copy(done, done, store_sems.at[j]).wait()


def reduce_all(wide_a, mlp_turned, gate_right, up_right, out_turned, act_right, gains):
    half = jax.ShapeDtypeStruct((480, 2560), jnp.bfloat16)
    half_turned = jax.ShapeDtypeStruct((960, 1280), jnp.bfloat16)
    count = len(CHUNKS)
    anywhere = pl.BlockSpec(memory_space=pl.ANY)
    near = pl.BlockSpec(memory_space=pltpu.VMEM)
    return pl.pallas_call(
        reduce_kernel,
        out_shape=(
            half, half, half, half_turned, jax.ShapeDtypeStruct(gains.shape, gains.dtype),
        ),
        in_specs=[anywhere] + [near] * 6,
        out_specs=(anywhere,) * 4 + (near,),
        scratch_shapes=[
            pltpu.VMEM((count,) + lead + (PIECE_ROWS, PIECE_COLUMNS), jnp.bfloat16)
            for lead in ((2, 2, 4), (2, 4), (4,), (2,), (), (), (2, 4))
        ] + [
            pltpu.VMEM((6,) + gains.shape, jnp.float32),
            pltpu.VMEM((5,) + gains.shape, jnp.float32),
            pltpu.SemaphoreType.DMA((count,)),
            pltpu.SemaphoreType.DMA((count,)),
            pltpu.SemaphoreType.DMA((8, count)),
            pltpu.SemaphoreType.DMA((8, count)),
            pltpu.SemaphoreType.DMA((2, 5)),
        ],
        compiler_params=pltpu.CompilerParams(
            collective_id=1, has_side_effects=True, vmem_limit_bytes=63 * 1024 * 1024
        ),
    )(wide_a, mlp_turned, gate_right, up_right, out_turned, act_right, gains)


def per_device(
    tokens,
    segments,
    cotangent,
    attn_gain,
    w_query,
    w_key,
    w_value,
    w_out,
    mlp_gain,
    w_gate,
    w_up,
    w_down,
    direct,
):
    if direct:
        attn_shard = jnp.concatenate([w_query, w_key, w_value, w_out], axis=1)
        gain_shard = jnp.pad(jnp.stack([attn_gain, mlp_gain]), ((0, 14), (0, 32)))
        attn_w, gate_w, up_w, down_turned, gains = gather_all(
            attn_shard, w_gate, w_up, w_down.T, gain_shard
        )
        gain_one = gains[:, 0, :480].reshape(-1)
        gain_two = gains[:, 1, :480].reshape(-1)
        qkv_w, out_w = attn_w[:, :1600], attn_w[:, 1600:]
    else:
        shards = (attn_gain, w_query, w_key, w_value, w_out, mlp_gain, w_gate, w_up, w_down)
        gain_one, query_w, key_w, value_w, out_w, gain_two, gate_w, up_w, down_w = [
            lax.all_gather(shard, "fsdp", axis=0, tiled=True) for shard in shards
        ]
        qkv_w = jnp.concatenate([query_w, key_w, value_w], axis=1)
        down_turned = down_w.T
    cosine, sine = rope_tables(segments)
    resid_in = tokens.astype(jnp.float32)
    normed_one, scale_one, attn_in = norm_forward(resid_in, gain_one)
    projected = product(attn_in, qkv_w)
    queries = rotate(projected[:, :960], cosine, sine, 1.0).astype(jnp.bfloat16)
    keys = rotate(projected[:, 960:1280], cosine, sine, 1.0).astype(jnp.bfloat16)
    values = projected[:, 1280:].astype(jnp.bfloat16)
    mixed, log_totals = attend_forward(queries, keys, values, segments)
    mixed_low = mixed.astype(jnp.bfloat16)
    middle = resid_in + product(mixed_low, out_w)
    normed_two, scale_two, mlp_in = norm_forward(middle, gain_two)
    gate = product(mlp_in, gate_w)
    upward = product(mlp_in, up_w)
    sigma = jax.nn.sigmoid(gate)
    activated = (gate * sigma * upward).astype(jnp.bfloat16)
    result = middle + product(activated, down_turned.T)
    grad_out = cotangent.astype(jnp.float32)
    grad_low = grad_out.astype(jnp.bfloat16)
    grad_act = product(grad_low, down_turned)
    grad_gate = (grad_act * upward * sigma * (1.0 + gate * (1.0 - sigma))).astype(jnp.bfloat16)
    grad_up = (grad_act * gate * sigma).astype(jnp.bfloat16)
    grad_mlp_in = product(grad_gate, gate_w.T) + product(grad_up, up_w.T)
    grad_norm_two, gain_two_grad = norm_backward(grad_mlp_in, normed_two, scale_two, gain_two)
    grad_middle = grad_out + grad_norm_two
    grad_middle_low = grad_middle.astype(jnp.bfloat16)
    out_grad = product(mixed_low.T, grad_middle_low)
    grad_mixed = product(grad_middle_low, out_w.T).astype(jnp.bfloat16)
    grad_queries, grad_keys, grad_values = attend_backward(
        queries, keys, values, grad_mixed, segments, log_totals
    )
    grad_query_pre = rotate(grad_queries, cosine, sine, -1.0).astype(jnp.bfloat16)
    grad_key_pre = rotate(grad_keys, cosine, sine, -1.0).astype(jnp.bfloat16)
    grad_value_pre = grad_values.astype(jnp.bfloat16)
    grad_qkv = jnp.concatenate([grad_query_pre, grad_key_pre, grad_value_pre], axis=1)
    qkv_grad = product(attn_in.T, grad_qkv)
    grad_attn_in = product(grad_qkv, qkv_w.T)
    grad_norm_one, gain_one_grad = norm_backward(grad_attn_in, normed_one, scale_one, gain_one)
    input_grad = grad_middle + grad_norm_one
    low = jnp.bfloat16
    attn_grad = jnp.concatenate([qkv_grad.astype(low), out_grad.astype(low)], axis=1)
    if direct:
        gain_rows = jnp.pad(jnp.stack([gain_one_grad, gain_two_grad]), ((0, 6), (0, 64)))
        attn_sum, gate_sum, up_sum, down_sum, gain_sum = reduce_all(
            attn_grad, mlp_in.T, grad_gate, grad_up, grad_low.T, activated, gain_rows
        )
        down_sum = down_sum.T
        at = lax.axis_index("fsdp") * 480
        gain_sums = [lax.dynamic_slice(gain_sum[i], (at,), (480,)) for i in range(2)]
    else:
        down_grad = product(activated.T, grad_low)
        gate_grad = product(mlp_in.T, grad_gate)
        up_grad = product(mlp_in.T, grad_up)
        partial = (down_grad, gate_grad, up_grad, attn_grad, gain_one_grad, gain_two_grad)
        sums = []
        for grad in partial:
            share = lax.psum_scatter(
                grad.astype(low), "fsdp", scatter_dimension=0, tiled=True
            )
            sums.append(lax.psum(share, "dp"))
        down_sum, gate_sum, up_sum, attn_sum = sums[:4]
        gain_sums = sums[4:]
    totals = (
        gain_sums[0], attn_sum[:, :960], attn_sum[:, 960:1280], attn_sum[:, 1280:1600],
        attn_sum[:, 1600:], gain_sums[1], gate_sum, up_sum, down_sum,
    )
    totals = [total.astype(jnp.float32) for total in totals]
    return (result.astype(jnp.bfloat16), input_grad) + tuple(totals)


def solution(mesh):
    in_specs = (
        P(("dp", "fsdp"), None),
        P(("dp", "fsdp")),
        P(("dp", "fsdp"), None),
        P("fsdp"),
        P("fsdp", None),
        P("fsdp", None),
        P("fsdp", None),
        P("fsdp", None),
        P("fsdp"),
        P("fsdp", None),
        P("fsdp", None),
        P("fsdp", None),
    )
    out_specs = (
        P(("dp", "fsdp"), None),
        P(("dp", "fsdp"), None),
        P("fsdp"),
        P("fsdp", None),
        P("fsdp", None),
        P("fsdp", None),
        P("fsdp", None),
        P("fsdp"),
        P("fsdp", None),
        P("fsdp", None),
        P("fsdp", None),
    )
    direct = mesh.shape["dp"] == 16 and mesh.shape["fsdp"] == 2
    return jax.shard_map(
        functools.partial(per_device, direct=direct), mesh=mesh, in_specs=in_specs, out_specs=out_specs, check_vma=False
    )
```

```python
import functools

import jax
import jax.numpy as jnp
from jax import lax
from jax.experimental import pallas as pl
from jax.experimental.pallas import tpu as pltpu
from jax.sharding import PartitionSpec as P

HEADS = 15
KV_HEADS = 5
HEAD = 64


epsilon = 1e-05
rope_base = 100000.0
masked_score = -1e30


def rope_tables(segment_ids):
    places = jnp.arange(segment_ids.shape[0], dtype=jnp.int32)
    changed = jnp.concatenate([jnp.ones((1,), dtype=bool), segment_ids[1:] != segment_ids[:-1]])
    first = lax.cummax(jnp.where(changed, places, 0), axis=0)
    position = (places - first).astype(jnp.float32)
    frequency = rope_base ** (-jnp.arange(0, HEAD, 2, dtype=jnp.float32) / HEAD)
    angles = position[:, None] * frequency[None, :]
    angles = jnp.concatenate([angles, angles], axis=1)
    return (jnp.cos(angles), jnp.sin(angles))


def rotate(values, cosine, sine, direction):
    rows_total = values.shape[0]
    shaped = values.reshape(rows_total, -1, HEAD)
    midway = HEAD // 2
    turned = jnp.concatenate([-shaped[..., midway:], shaped[..., :midway]], axis=-1)
    return (shaped * cosine[:, None, :] + direction * turned * sine[:, None, :]).reshape(
        rows_total, -1
    )


def norm_forward(values, gain):
    scale_rows = lax.rsqrt(jnp.mean(values * values, axis=-1, keepdims=True) + epsilon)
    normed = values * scale_rows
    return (normed, scale_rows, (normed * gain.astype(jnp.float32)).astype(jnp.bfloat16))


def norm_backward(grad_scaled, normed, scale_rows, gain):
    gain_grad = jnp.sum(grad_scaled * normed, axis=0)
    grad_normed = grad_scaled * gain.astype(jnp.float32)
    inner = jnp.mean(grad_normed * normed, axis=-1, keepdims=True)
    return (scale_rows * (grad_normed - normed * inner), gain_grad)


def block_mask(segment_ids, first_row, last_row):
    places = jnp.arange(segment_ids.shape[0])
    same = segment_ids[first_row:last_row, None] == segment_ids[None, :last_row]
    causal = places[first_row:last_row, None] >= places[None, :last_row]
    return same & causal


def block_scores(query_block, key_block, allowed):
    scores = jnp.einsum(
        "qrd,kd->rqk", query_block, key_block, preferred_element_type=jnp.float32
    ) * HEAD ** (-0.5)
    return jnp.where(allowed[None], scores, masked_score)


def attend_forward(queries, keys, values, segment_ids):
    rows_total = queries.shape[0]
    block_rows = min(512, rows_total)
    group = HEADS // KV_HEADS
    log_totals = []
    allowed = block_mask(segment_ids, 0, block_rows)
    head_parts = []
    for kv_index in range(KV_HEADS):
        query_block = queries[0:block_rows, kv_index * group * HEAD : (kv_index + 1) * group * HEAD]
        query_block = query_block.reshape(block_rows, group, HEAD)
        key_block = keys[:block_rows, kv_index * HEAD : (kv_index + 1) * HEAD]
        value_block = values[:block_rows, kv_index * HEAD : (kv_index + 1) * HEAD]
        scores = block_scores(query_block, key_block, allowed)
        highest = jnp.max(scores, axis=-1, keepdims=True)
        exponent = jnp.exp(scores - highest)
        totals = jnp.sum(exponent, axis=-1, keepdims=True)
        probability = (exponent / totals).astype(jnp.bfloat16)
        log_totals.append(highest + jnp.log(totals))
        mixed = jnp.einsum(
            "rqk,kd->qrd", probability, value_block, preferred_element_type=jnp.float32
        )
        head_parts.append(mixed.reshape(block_rows, group * HEAD))
    mixed_rows = jnp.concatenate(head_parts, axis=1)
    return (mixed_rows, log_totals)


def attend_backward(queries, keys, values, grad_mixed, segment_ids, log_totals):
    rows_total = queries.shape[0]
    block_rows = min(512, rows_total)
    group = HEADS // KV_HEADS
    key_grads = [jnp.zeros((rows_total, HEAD), jnp.float32) for kv_index in range(KV_HEADS)]
    value_grads = [jnp.zeros((rows_total, HEAD), jnp.float32) for kv_index in range(KV_HEADS)]
    entry = 0
    allowed = block_mask(segment_ids, 0, block_rows)
    head_parts = []
    for kv_index in range(KV_HEADS):
        columns_lo = kv_index * group * HEAD
        columns_hi = (kv_index + 1) * group * HEAD
        query_block = queries[0:block_rows, columns_lo:columns_hi].reshape(block_rows, group, HEAD)
        grad_block = grad_mixed[0:block_rows, columns_lo:columns_hi].reshape(
            block_rows, group, HEAD
        )
        key_block = keys[:block_rows, kv_index * HEAD : (kv_index + 1) * HEAD]
        value_block = values[:block_rows, kv_index * HEAD : (kv_index + 1) * HEAD]
        scores = block_scores(query_block, key_block, allowed)
        probability = jnp.exp(scores - log_totals[entry])
        entry = entry + 1
        grad_prob = jnp.einsum(
            "qrd,kd->rqk", grad_block, value_block, preferred_element_type=jnp.float32
        )
        weighted = jnp.sum(probability * grad_prob, axis=-1, keepdims=True)
        grad_scores = (probability * (grad_prob - weighted)).astype(jnp.bfloat16)
        grad_query = jnp.einsum(
            "rqk,kd->qrd", grad_scores, key_block, preferred_element_type=jnp.float32
        ) * HEAD ** (-0.5)
        head_parts.append(grad_query.reshape(block_rows, group * HEAD))
        grad_key = jnp.einsum(
            "rqk,qrd->kd", grad_scores, query_block, preferred_element_type=jnp.float32
        ) * HEAD ** (-0.5)
        grad_value = jnp.einsum(
            "rqk,qrd->kd",
            probability.astype(jnp.bfloat16),
            grad_block,
            preferred_element_type=jnp.float32,
        )
        key_grads[kv_index] = grad_key
        value_grads[kv_index] = grad_value
    grad_query_rows = jnp.concatenate(head_parts, axis=1)
    return (
        grad_query_rows,
        jnp.concatenate(key_grads, axis=1),
        jnp.concatenate(value_grads, axis=1),
    )


def product(left, right):
    return jnp.dot(left, right, preferred_element_type=jnp.float32)


MESH = pl.DeviceIdType.MESH
CUTS = 3
PIECE_ROWS = 80
PIECE_COLUMNS = 640
CHUNKS = [(which, cut) for which in range(4) for cut in range(CUTS)]


def place():
    dp = lax.axis_index("dp")
    fs = lax.axis_index("fsdp")
    bits = [lax.rem(lax.div(dp, 1 << shift), 2) for shift in range(4)]
    flips = [dp + (1 << shift) - (2 << shift) * bits[shift] for shift in range(4)]
    across = (dp, 1 - fs)
    core, along_y, near_z, far_z = [(flip, fs) for flip in flips]
    return fs, bits, across, core, along_y, near_z, far_z


def greet(partners):
    barrier = pltpu.get_barrier_semaphore()
    for partner in partners:
        pl.semaphore_signal(barrier, inc=1, device_id=partner, device_id_type=MESH)
    pl.semaphore_wait(barrier, len(partners))


def aligned(value, unit):
    return pl.multiple_of(value, unit)


def piece(ref, which, cut, shard, half, q):
    if which == 3:
        rows = (cut * 4 + half * 2 + q // 2) * PIECE_ROWS
        columns = shard * 1280 + (q % 2) * PIECE_COLUMNS
    else:
        rows = shard * 480 + (cut * 2 + half) * PIECE_ROWS
        columns = q * PIECE_COLUMNS
    rows, columns = aligned(rows, 16), aligned(columns, 128)
    return ref.at[pl.ds(rows, PIECE_ROWS), pl.ds(columns, PIECE_COLUMNS)]


def gather_kernel(
    wide_a, wide_b, wide_c, turned, gains,
    full_a, full_b, full_c, full_turned, full_gains,
    held_wide, held_turned, got,
    load_sems, keep_sems, store_sems, gain_sem, send_sems, recv_sems,
):
    fs, bits, across, core, along_y, near_z, _ = place()
    c, y, z = bits[0], bits[1], bits[2]
    shards = (wide_a, wide_b, wide_c, turned)
    fulls = (full_a, full_b, full_c, full_turned)
    count = len(CHUNKS)

    def send(src, dst, stage, index, target):
        copy = pltpu.make_async_remote_copy(
            src_ref=src, dst_ref=dst, send_sem=send_sems.at[stage, index],
            recv_sem=recv_sems.at[stage, index], device_id=target, device_id_type=MESH,
        )
        copy.start()
        return copy

    loads, keeps = [], []
    for j, (which, cut) in enumerate(CHUNKS):
        if which == 3:
            held = held_turned.at[cut]
            src = turned.at[pl.ds(cut * 320, 320), :]
            dst = full_turned.at[pl.ds(cut * 320, 320), pl.ds(aligned(fs * 1280, 128), 1280)]
        else:
            held = held_wide.at[3 * which + cut]
            src = shards[which].at[pl.ds(cut * 160, 160), :]
            dst = fulls[which].at[pl.ds(aligned(fs * 480 + cut * 160, 16), 160), :]
        loads.append(pltpu.make_async_copy(src, held, load_sems.at[j]))
        keeps.append(pltpu.make_async_copy(held, dst, keep_sems.at[j]))
        loads[j].start()
    keep_gains = pltpu.make_async_copy(gains, full_gains.at[fs], gain_sem)
    keep_gains.start()
    greet((across, core, along_y, near_z))
    gain_copy = send(gains, full_gains.at[fs], 0, count, across)
    copies = [[None] * count for _ in range(4)]

    def lead(j):
        return (y, z) if j % 2 == 0 else (z, y)

    for j, (which, cut) in enumerate(CHUNKS):
        first, second = lead(j)
        loads[j].wait()
        q = 2 * first + second
        if which == 3:
            src = held_turned.at[
                cut, pl.ds(aligned((2 * c + first) * PIECE_ROWS, 16), PIECE_ROWS),
                pl.ds(aligned(second * PIECE_COLUMNS, 128), PIECE_COLUMNS),
            ]
        else:
            src = held_wide.at[
                3 * which + cut, pl.ds(aligned(c * PIECE_ROWS, 16), PIECE_ROWS),
                pl.ds(aligned(q * PIECE_COLUMNS, 128), PIECE_COLUMNS),
            ]
        copies[0][j] = send(src, got.at[j, c, q], 0, j, across)
        keeps[j].start()

    def forward_one(j):
        first, second = lead(j)
        copies[0][j].wait_recv()
        part = got.at[j, c, 2 * first + second]
        copies[1][j] = send(part, part, 1, j, near_z if j % 2 == 0 else along_y)

    def forward_two(j):
        first, _ = lead(j)
        copies[1][j].wait_recv()
        part = got.at[j, c, pl.ds(2 * first, 2)]
        copies[2][j] = send(part, part, 2, j, along_y if j % 2 == 0 else near_z)

    def forward_four(j):
        copies[2][j].wait_recv()
        copies[3][j] = send(got.at[j, c], got.at[j, c], 3, j, core)

    def store(j):
        which, cut = CHUNKS[j]
        copies[3][j].wait_recv()
        for half in range(2):
            for q in range(4):
                pltpu.make_async_copy(
                    got.at[j, half, q], piece(fulls[which], which, cut, 1 - fs, half, q),
                    store_sems.at[j],
                ).start()

    stages = (forward_one, forward_two, forward_four, store)
    for step in range(count + len(stages) - 1):
        for late, stage in enumerate(stages):
            if 0 <= step - late < count:
                stage(step - late)
    gain_copy.wait()
    keep_gains.wait()
    for j in range(count):
        keeps[j].wait()
        pltpu.make_async_copy(got.at[j], got.at[j], store_sems.at[j]).wait()
    for row in copies:
        for copy in row:
            copy.wait_send()


def gather_all(wide_a, wide_b, wide_c, turned, gains):
    full = jax.ShapeDtypeStruct((960, 2560), jnp.bfloat16)
    anywhere = pl.BlockSpec(memory_space=pl.ANY)
    count = len(CHUNKS)
    return pl.pallas_call(
        gather_kernel,
        out_shape=(full,) * 4 + (jax.ShapeDtypeStruct((2,) + gains.shape, gains.dtype),),
        in_specs=[anywhere] * 5,
        out_specs=(anywhere,) * 5,
        scratch_shapes=[
            pltpu.VMEM((9, 160, 2560), jnp.bfloat16),
            pltpu.VMEM((3, 320, 1280), jnp.bfloat16),
            pltpu.VMEM((count, 2, 4, PIECE_ROWS, PIECE_COLUMNS), jnp.bfloat16),
            pltpu.SemaphoreType.DMA((count,)),
            pltpu.SemaphoreType.DMA((count,)),
            pltpu.SemaphoreType.DMA((count,)),
            pltpu.SemaphoreType.DMA,
            pltpu.SemaphoreType.DMA((4, count + 1)),
            pltpu.SemaphoreType.DMA((4, count + 1)),
        ],
        compiler_params=pltpu.CompilerParams(
            collective_id=0, has_side_effects=True, vmem_limit_bytes=60 * 1024 * 1024
        ),
    )(wide_a, wide_b, wide_c, turned, gains)


def reduce_kernel(
    wide_a, wide_b, wide_c, turned, gains,
    sum_a, sum_b, sum_c, sum_turned, sum_gains,
    own_all, core_all, across_all, y_all, near_all, far_all, done_all,
    gain_acc, gain_got, load_sems, store_sems, send_sems, recv_sems, gain_sems,
):
    fs, bits, across, core, along_y, near_z, far_z = place()
    c, y, z = bits[0], bits[1], bits[2]
    mine = 2 * y + z
    sources = (wide_a, wide_b, wide_c, turned)
    sinks = (sum_a, sum_b, sum_c, sum_turned)
    chunks = CHUNKS[::-1]
    count = len(chunks)
    scratches = (own_all, core_all, across_all, y_all, near_all, far_all, done_all)
    held = [[ref.at[j] for ref in scratches] for j in range(count)]

    def send(src, dst, stage, j, target):
        copy = pltpu.make_async_remote_copy(
            src_ref=src, dst_ref=dst, send_sem=send_sems.at[stage, j],
            recv_sem=recv_sems.at[stage, j], device_id=target, device_id_type=MESH,
        )
        copy.start()
        return copy

    def add_into(dst, src, total):
        def body(i, carry):
            left = dst[i].astype(jnp.float32)
            dst[i] = (left + src[i].astype(jnp.float32)).astype(jnp.bfloat16)
            return carry

        lax.fori_loop(0, total, body, 0)

    for j, (which, cut) in enumerate(chunks):
        for half in range(2):
            for shard in range(2):
                for q in range(4):
                    pltpu.make_async_copy(
                        piece(sources[which], which, cut, shard, half, q),
                        held[j][0].at[half, shard, q], load_sems.at[j],
                    ).start()
    gain_acc[0] = gains[...]
    greet((across, core, along_y, near_z, far_z))

    partners = (core, across, along_y, near_z, far_z)
    gain_copies = []

    def gain_send(i):
        copy = pltpu.make_async_remote_copy(
            src_ref=gain_acc.at[i], dst_ref=gain_got.at[i], send_sem=gain_sems.at[0, i],
            recv_sem=gain_sems.at[1, i], device_id=partners[i], device_id_type=MESH,
        )
        copy.start()
        gain_copies.append(copy)

    def gain_step(i):
        gain_copies[i].wait_recv()
        gain_acc[i + 1] = gain_acc[i] + gain_got[i]
        if i < 4:
            gain_send(i + 1)

    copies = [[None] * count for _ in range(8)]
    gain_send(0)
    def stage_zero(j):
        whole = held[j][0]
        pltpu.make_async_copy(whole, whole, load_sems.at[j]).wait()
        copies[0][j] = send(whole.at[1 - c], held[j][1], 0, j, core)

    def stage_one(j):
        own, got = held[j][0], held[j][1]
        copies[0][j].wait_recv()
        add_into(own.at[c, 1 - fs], got.at[1 - fs], 4)
        copies[1][j] = send(own.at[c, 1 - fs], held[j][2], 1, j, across)
        add_into(own.at[c, fs], got.at[fs], 4)

    for step in range(count + 2):
        if step < count:
            stage_zero(step)
        if step >= 2:
            stage_one(step - 2)
    gain_step(0)

    def stage_two(j):
        own = held[j][0]
        copies[1][j].wait_recv()
        add_into(own.at[c, fs], held[j][2], 4)
        copies[2][j] = send(
            own.at[c, fs, pl.ds(2 * (1 - y), 2)], held[j][3], 2, j, along_y
        )

    def stage_three(j):
        own = held[j][0]
        copies[2][j].wait_recv()
        add_into(own.at[c, fs, pl.ds(2 * y, 2)], held[j][3], 2)
        copies[3][j] = send(own.at[c, fs, 2 * y + 1 - z], held[j][4], 3, j, near_z)

    def stage_four(j):
        own = held[j][0]
        copies[3][j].wait_recv()
        left = own[c, fs, mine].astype(jnp.float32)
        own[c, fs, mine] = (left + held[j][4][...].astype(jnp.float32)).astype(jnp.bfloat16)
        copies[4][j] = send(own.at[c, fs, mine], held[j][5], 4, j, far_z)

    def stage_five(j):
        own, done = held[j][0], held[j][6]
        copies[4][j].wait_recv()
        left = own[c, fs, mine].astype(jnp.float32)
        done[c, mine] = (left + held[j][5][...].astype(jnp.float32)).astype(jnp.bfloat16)
        copies[5][j] = send(done.at[c, mine], done.at[c, mine], 5, j, near_z)

    def stage_six(j):
        done = held[j][6]
        copies[5][j].wait_recv()
        pair = done.at[c, pl.ds(2 * y, 2)]
        copies[6][j] = send(pair, pair, 6, j, along_y)

    def stage_seven(j):
        done = held[j][6]
        copies[6][j].wait_recv()
        copies[7][j] = send(done.at[c], done.at[c], 7, j, core)

    def stage_eight(j):
        done = held[j][6]
        which, cut = chunks[j]
        copies[7][j].wait_recv()
        for half in range(2):
            for q in range(4):
                pltpu.make_async_copy(
                    done.at[half, q], piece(sinks[which], which, cut, 0, half, q),
                    store_sems.at[j],
                ).start()

    order = (
        (stage_two, 0), (stage_four, 1), (stage_six, 2), (stage_eight, 3),
        (stage_three, 0), (stage_five, 1), (stage_seven, 2),
    )
    for step in range(count + 3):
        for stage, late in order:
            if 0 <= step - late < count:
                stage(step - late)
        if step < 4:
            gain_step(step + 1)
    sum_gains[...] = gain_acc[5]
    for row in copies:
        for copy in row:
            copy.wait_send()
    for copy in gain_copies:
        copy.wait_send()
    for j in range(count):
        done = held[j][6]
        pltpu.make_async_copy(done, done, store_sems.at[j]).wait()


def reduce_all(wide_a, wide_b, wide_c, turned, gains):
    half = jax.ShapeDtypeStruct((480, 2560), jnp.bfloat16)
    half_turned = jax.ShapeDtypeStruct((960, 1280), jnp.bfloat16)
    count = len(CHUNKS)
    anywhere = pl.BlockSpec(memory_space=pl.ANY)
    near = pl.BlockSpec(memory_space=pltpu.VMEM)
    return pl.pallas_call(
        reduce_kernel,
        out_shape=(
            half, half, half, half_turned, jax.ShapeDtypeStruct(gains.shape, gains.dtype),
        ),
        in_specs=[anywhere] * 4 + [near],
        out_specs=(anywhere,) * 4 + (near,),
        scratch_shapes=[
            pltpu.VMEM((count,) + lead + (PIECE_ROWS, PIECE_COLUMNS), jnp.bfloat16)
            for lead in ((2, 2, 4), (2, 4), (4,), (2,), (), (), (2, 4))
        ] + [
            pltpu.VMEM((6,) + gains.shape, jnp.float32),
            pltpu.VMEM((5,) + gains.shape, jnp.float32),
            pltpu.SemaphoreType.DMA((count,)),
            pltpu.SemaphoreType.DMA((count,)),
            pltpu.SemaphoreType.DMA((8, count)),
            pltpu.SemaphoreType.DMA((8, count)),
            pltpu.SemaphoreType.DMA((2, 5)),
        ],
        compiler_params=pltpu.CompilerParams(
            collective_id=1, has_side_effects=True, vmem_limit_bytes=60 * 1024 * 1024
        ),
    )(wide_a, wide_b, wide_c, turned, gains)


def per_device(
    tokens,
    segments,
    cotangent,
    attn_gain,
    w_query,
    w_key,
    w_value,
    w_out,
    mlp_gain,
    w_gate,
    w_up,
    w_down,
    direct,
):
    if direct:
        attn_shard = jnp.concatenate([w_query, w_key, w_value, w_out], axis=1)
        gain_shard = jnp.pad(jnp.stack([attn_gain, mlp_gain]), ((0, 14), (0, 32)))
        attn_w, gate_w, up_w, down_turned, gains = gather_all(
            attn_shard, w_gate, w_up, w_down.T, gain_shard
        )
        gain_one = gains[:, 0, :480].reshape(-1)
        gain_two = gains[:, 1, :480].reshape(-1)
        qkv_w, out_w = attn_w[:, :1600], attn_w[:, 1600:]
    else:
        shards = (attn_gain, w_query, w_key, w_value, w_out, mlp_gain, w_gate, w_up, w_down)
        gain_one, query_w, key_w, value_w, out_w, gain_two, gate_w, up_w, down_w = [
            lax.all_gather(shard, "fsdp", axis=0, tiled=True) for shard in shards
        ]
        qkv_w = jnp.concatenate([query_w, key_w, value_w], axis=1)
        down_turned = down_w.T
    cosine, sine = rope_tables(segments)
    resid_in = tokens.astype(jnp.float32)
    normed_one, scale_one, attn_in = norm_forward(resid_in, gain_one)
    projected = product(attn_in, qkv_w)
    queries = rotate(projected[:, :960], cosine, sine, 1.0).astype(jnp.bfloat16)
    keys = rotate(projected[:, 960:1280], cosine, sine, 1.0).astype(jnp.bfloat16)
    values = projected[:, 1280:].astype(jnp.bfloat16)
    mixed, log_totals = attend_forward(queries, keys, values, segments)
    mixed_low = mixed.astype(jnp.bfloat16)
    middle = resid_in + product(mixed_low, out_w)
    normed_two, scale_two, mlp_in = norm_forward(middle, gain_two)
    gate = product(mlp_in, gate_w)
    upward = product(mlp_in, up_w)
    sigma = jax.nn.sigmoid(gate)
    activated = (gate * sigma * upward).astype(jnp.bfloat16)
    result = middle + product(activated, down_turned.T)
    grad_out = cotangent.astype(jnp.float32)
    grad_low = grad_out.astype(jnp.bfloat16)
    down_grad = product(grad_low.T, activated)
    grad_act = product(grad_low, down_turned)
    grad_gate = (grad_act * upward * sigma * (1.0 + gate * (1.0 - sigma))).astype(jnp.bfloat16)
    grad_up = (grad_act * gate * sigma).astype(jnp.bfloat16)
    gate_grad = product(mlp_in.T, grad_gate)
    up_grad = product(mlp_in.T, grad_up)
    grad_mlp_in = product(grad_gate, gate_w.T) + product(grad_up, up_w.T)
    grad_norm_two, gain_two_grad = norm_backward(grad_mlp_in, normed_two, scale_two, gain_two)
    grad_middle = grad_out + grad_norm_two
    grad_middle_low = grad_middle.astype(jnp.bfloat16)
    out_grad = product(mixed_low.T, grad_middle_low)
    grad_mixed = product(grad_middle_low, out_w.T).astype(jnp.bfloat16)
    grad_queries, grad_keys, grad_values = attend_backward(
        queries, keys, values, grad_mixed, segments, log_totals
    )
    grad_query_pre = rotate(grad_queries, cosine, sine, -1.0).astype(jnp.bfloat16)
    grad_key_pre = rotate(grad_keys, cosine, sine, -1.0).astype(jnp.bfloat16)
    grad_value_pre = grad_values.astype(jnp.bfloat16)
    grad_qkv = jnp.concatenate([grad_query_pre, grad_key_pre, grad_value_pre], axis=1)
    qkv_grad = product(attn_in.T, grad_qkv)
    grad_attn_in = product(grad_qkv, qkv_w.T)
    grad_norm_one, gain_one_grad = norm_backward(grad_attn_in, normed_one, scale_one, gain_one)
    input_grad = grad_middle + grad_norm_one
    low = jnp.bfloat16
    attn_grad = jnp.concatenate([qkv_grad.astype(low), out_grad.astype(low)], axis=1)
    if direct:
        gain_rows = jnp.pad(jnp.stack([gain_one_grad, gain_two_grad]), ((0, 6), (0, 64)))
        attn_sum, gate_sum, up_sum, down_sum, gain_sum = reduce_all(
            attn_grad, gate_grad.astype(low), up_grad.astype(low), down_grad.astype(low),
            gain_rows,
        )
        down_sum = down_sum.T
        at = lax.axis_index("fsdp") * 480
        gain_sums = [lax.dynamic_slice(gain_sum[i], (at,), (480,)) for i in range(2)]
    else:
        partial = (down_grad.T, gate_grad, up_grad, attn_grad, gain_one_grad, gain_two_grad)
        sums = []
        for grad in partial:
            share = lax.psum_scatter(
                grad.astype(low), "fsdp", scatter_dimension=0, tiled=True
            )
            sums.append(lax.psum(share, "dp"))
        down_sum, gate_sum, up_sum, attn_sum = sums[:4]
        gain_sums = sums[4:]
    totals = (
        gain_sums[0], attn_sum[:, :960], attn_sum[:, 960:1280], attn_sum[:, 1280:1600],
        attn_sum[:, 1600:], gain_sums[1], gate_sum, up_sum, down_sum,
    )
    totals = [total.astype(jnp.float32) for total in totals]
    return (result.astype(jnp.bfloat16), input_grad) + tuple(totals)


def solution(mesh):
    in_specs = (
        P(("dp", "fsdp"), None),
        P(("dp", "fsdp")),
        P(("dp", "fsdp"), None),
        P("fsdp"),
        P("fsdp", None),
        P("fsdp", None),
        P("fsdp", None),
        P("fsdp", None),
        P("fsdp"),
        P("fsdp", None),
        P("fsdp", None),
        P("fsdp", None),
    )
    out_specs = (
        P(("dp", "fsdp"), None),
        P(("dp", "fsdp"), None),
        P("fsdp"),
        P("fsdp", None),
        P("fsdp", None),
        P("fsdp", None),
        P("fsdp", None),
        P("fsdp"),
        P("fsdp", None),
        P("fsdp", None),
        P("fsdp", None),
    )
    direct = mesh.shape["dp"] == 16 and mesh.shape["fsdp"] == 2
    return jax.shard_map(
        functools.partial(per_device, direct=direct), mesh=mesh, in_specs=in_specs, out_specs=out_specs, check_vma=False
    )
```
